512 devices in a mesh: pw: 8 (over x, y_lo), pair: 64 (over y_hi, z, core).
Axes of the slice: x: 4, y: 8 (y_hi: 4, y_lo: 2; y = y_hi * 2 + y_lo), z: 8, core: 2. Of those that a mesh axis runs over, the one named last changes fastest.
Arguments:
- valence_pairs: bfloat16 [64, 64, 8192], P('pair', None, 'pw'), may hold values from -0.59765625 to 0.59765625
- conduction_pairs: bfloat16 [64, 256, 8192], P('pair', None, 'pw'), may hold values from -0.59765625 to 0.59765625
- screening: float32 [8192], P('pw'), may hold values from 0.1 to 2
Outputs:
- kernel: float32 [64, 64, 64, 256], P('pair', None, 'pw')
The draws below stay inside these ranges and needn't reach their ends.
All inputs are finite; a program needn't handle non-finite values.
Results may differ from the reference program's by a relative error of at most 0.0029.
Values may be sent and summed in bfloat16 or wider, within the bound.
No kernel may reach another device: no remote copies, remote signals or barrier semaphores. Data moves between devices by JAX's collectives and lax.ppermute only.
A program may use at most 64 MiB of HBM per device.

```python
import math
import jax
import jax.numpy as jnp
from jax import lax

V = 64
C = 256
G = 8192
CS = 64


def raised(entries, own_key, source, target, shards_of, factor):
    owner, partner = [(jnp.arange(entries.shape[dim]) // (entries.shape[dim] // shards_of)).reshape([-1 if axis == dim else 1 for axis in range(entries.ndim)]) for dim in (source, target)]
    chosen = jax.random.permutation(own_key, shards_of)[partner]
    strong = (owner == chosen) | (owner == (partner + shards_of // 2) % shards_of)
    return jnp.where(strong, factor * entries, entries)


def levels(stream_key, shape, shards, least, largest):
    gain = 1.0
    for dim, parts in shards:
        draws = jax.random.uniform(jax.random.fold_in(jax.random.fold_in(stream_key, 6), dim), (parts,), jnp.float32, least / len(shards), largest / len(shards))
        gain = gain * jnp.repeat(jnp.exp(draws), shape[dim] // parts).reshape((-1,) + (1,) * (len(shape) - 1 - dim))
    return gain


def gaussian(rng, dims, spread, most, pieces=(), held_as=jnp.bfloat16):
    array = jax.random.normal(rng, dims, jnp.float32) * spread
    if len(pieces) > 0:
        array = levels(rng, dims, pieces, -0.22, 0.18) * array
    return jnp.clip(array, min=-most, max=most).astype(held_as)


def heavy_noise(key, dims, scale, limit, split, heavy, held_as=jnp.bfloat16):
    entries = scale * jax.random.normal(key, dims, jnp.float32)
    if split:
        entries = entries * levels(key, dims, split, -0.22, 0.18)
    return jnp.clip(raised(entries, jax.random.fold_in(key, 3), *heavy), -limit, limit).astype(held_as)


def setup_inputs(seed: int = 0) -> dict:
    streams_of = jax.random.split(jax.random.key(seed), 4)
    valence_pairs = heavy_noise(streams_of[0], (V, V, G), 0.1, 0.59765625, ((0, 64), (2, 8)), (2, 1, 8, 2.0))
    conduction_pairs = gaussian(streams_of[1], (CS, C, G), 0.1, 0.59765625, ((0, 64), (2, 8)))
    screening = jnp.clip(jnp.exp(math.log(2.0) - 2.9957323 * jax.random.uniform(streams_of[2], (G,), jnp.float32) ** levels(streams_of[2], (G,), ((0, 8),), -0.2, 0.2)), 0.1, 2.0)
    return {"valence_pairs": valence_pairs, "conduction_pairs": conduction_pairs, "screening": screening}


def reference(valence_pairs, conduction_pairs, screening):
    screened = (valence_pairs.astype(jnp.float32) * screening[None, None, :]).astype(jnp.bfloat16)
    left = screened.astype(jnp.float32).reshape(V * V, G)
    right = conduction_pairs.astype(jnp.float32).reshape(CS * C, G)
    product = lax.dot_general(left, right, (((1,), (1,)), ((), ())), preferred_element_type=jnp.float32)
    return product.reshape(V, V, CS, C).transpose(0, 2, 1, 3)
```

```python
import functools

import jax
import jax.numpy as jnp
from jax import lax
from jax.experimental import pallas as pl
from jax.experimental.pallas import tpu as pltpu
from jax.sharding import Mesh, PartitionSpec as P

BF16 = jnp.bfloat16
F32 = jnp.float32
AXES = ("x", "yl", "yh", "z", "core")
SIZES = (4, 2, 4, 8, 2)
NX, NL, NH, NZ, NC = SIZES


def place(y):
    return (y % NL) * NH + y // NL


def intra(block):
    return lax.ppermute(block, "yl", [(0, 1), (1, 0)])


def inter(block):
    ny = NL * NH
    pairs = []
    for j in range(NH):
        a, b = place(2 * j + 1), place((2 * j + 2) % ny)
        pairs += [(a, b), (b, a)]
    return lax.ppermute(block, ("yl", "yh"), pairs)


def dot(left, right):
    return lax.dot_general(left, right, (((1,), (1,)), ((), ())), preferred_element_type=F32)


def product_kernel(parts, mine_ref, other_ref, *refs):
    rights, out_ref = refs[:-1], refs[-1]
    yl, core = lax.axis_index("yl"), lax.axis_index("core")
    _, nz, rows, width = mine_ref.shape
    nx = NX
    wide = rows // nx
    for which, ref in enumerate((mine_ref, other_ref)):
        target_core = core if which == 0 else 1 - core
        left = {h: ref[yl if h == 0 else 1 - yl].reshape(nz * rows, width) for h in (0, 1)}
        sums = []
        for slot in parts:
            pieces = {}
            for half, index, start in slot:
                pieces.setdefault(start, []).append(dot(left[half], rights[index][...]))
            sums.append(pieces)
        done = []
        for pieces in sums:
            whole = [sum(p[1:], p[0]) for p in (pieces[k] for k in sorted(pieces, key=str) if k is None)]
            halves = [k for k in sorted(k for k in pieces if k is not None)]
            total = whole[0] if whole else None
            if halves:
                joined = jnp.concatenate([pieces[k][0] for k in halves], axis=1)
                total = joined if total is None else total + joined
            done.append(total)
        for zi in range(nz):
            for xi in range(nx):
                at = zi * rows + xi * wide
                block = jnp.concatenate([d[at : at + wide] for d in done], axis=0)
                out_ref[(xi * nz + zi) * NC + target_core] = block.astype(BF16)


def product(mine, other, rights, parts):
    _, nz, rows, width = mine.shape
    wide = rows // NX
    columns = 256
    members = NX * nz * NC
    flops = 2 * 2 * nz * rows * width * 2 * columns * 2
    return pl.pallas_call(
        functools.partial(product_kernel, parts),
        out_shape=jax.ShapeDtypeStruct((members, 2 * wide, columns), BF16),
        in_specs=[pl.BlockSpec(memory_space=pltpu.VMEM)] * (2 + len(rights)),
        out_specs=pl.BlockSpec(memory_space=pltpu.VMEM),
        compiler_params=pltpu.CompilerParams(vmem_limit_bytes=16 * 1024 * 1024),
        cost_estimate=pl.CostEstimate(flops=flops, bytes_accessed=5 * 2**20, transcendentals=0),
    )(mine, other, *rights)


def finish_kernel(first_ref, second_ref, out_ref):
    yh = lax.axis_index("yh")
    step = 1 - 2 * lax.axis_index("yl")
    owners = [lax.rem(yh + NH + k, NH) for k in (0, -step, step, 2)]
    for which, ref in enumerate((first_ref, second_ref)):
        total = ref[0].astype(F32)
        for xi in range(1, NX):
            total = total + ref[xi].astype(F32)
        wide = total.shape[1] // 2
        out_ref[owners[2 * which]] = total[:, :wide]
        out_ref[owners[2 * which + 1]] = total[:, wide:]


def finish(first, second):
    members, tall, columns = first.shape
    rest = members // NX
    first = first.reshape(NX, rest, tall, columns)
    second = second.reshape(NX, rest, tall, columns)
    step = 4
    spec = pl.BlockSpec((NX, step, tall, columns), lambda i: (0, i, 0, 0))
    return pl.pallas_call(
        finish_kernel,
        grid=(rest // step,),
        out_shape=jax.ShapeDtypeStruct((NH, rest, tall // 2, columns), F32),
        in_specs=[spec, spec],
        out_specs=pl.BlockSpec((NH, step, tall // 2, columns), lambda i: (0, i, 0, 0)),
        cost_estimate=pl.CostEstimate(flops=2**19, bytes_accessed=3 * 2**19, transcendentals=0),
    )(first, second)


def body(valence_pairs, conduction_pairs, screening):
    _, second, plane_dev = valence_pairs.shape
    own = conduction_pairs[0]
    half = own.shape[0] // 2

    screened = (valence_pairs[0].astype(F32) * screening[None, :]).astype(BF16)
    wide = second // (NX * NL)
    by_half = screened.reshape(NX, NL, wide, plane_dev).transpose(1, 0, 2, 3)
    by_half = by_half.reshape(NL, 1, NX * wide, plane_dev)
    sent = jnp.broadcast_to(by_half, (NL, NZ, NX * wide, plane_dev))
    sent = sent.reshape(NL * NZ, NX * wide, plane_dev)
    mine = lax.all_to_all(sent, ("yl", "z"), 0, 0, tiled=True)
    f1, b1 = intra(own), inter(own)
    f2, b2 = intra(b1), inter(f1)
    mine, _, _ = lax.optimization_barrier((mine, f2, b2))
    other = lax.ppermute(mine, "core", [(0, 1), (1, 0)])
    mine = mine.reshape(NL, NZ, NX * wide, plane_dev)
    other = other.reshape(NL, NZ, NX * wide, plane_dev)
    f3, b3 = intra(b2), inter(f2)
    g4, h4 = intra(b3[:half]), inter(f3[half:])

    mine, other, _, _ = lax.optimization_barrier((mine, other, f3, b3))
    first = product(
        mine, other, (own, f1, b1, b2),
        (((0, 0, None), (1, 1, None)), ((1, 2, None), (0, 3, None))),
    )
    first = lax.all_to_all(first, ("x", "z", "core"), 0, 0, tiled=True)
    last = product(
        mine, other, (f2, f3, b3, g4, h4),
        (((0, 0, None), (1, 1, None)), ((1, 2, None), (0, 3, 0), (0, 4, 1))),
    )
    last = lax.all_to_all(last, ("x", "z", "core"), 0, 0, tiled=True)
    out = finish(first, last)
    return out.reshape(1, NH * NZ * NC, wide, own.shape[0])


def solution(mesh):
    fine = Mesh(mesh.devices.reshape(SIZES), AXES)
    pair, pw = ("yh", "z", "core"), ("x", "yl")
    placed = (P(pair, None, pw), P(pair, None, pw), P(pw))
    return jax.shard_map(
        body, mesh=fine, in_specs=placed, out_specs=P(pair, None, pw, None), check_vma=False
    )
```

```python
import functools

import jax
import jax.numpy as jnp
from jax import lax
from jax.experimental import pallas as pl
from jax.experimental.pallas import tpu as pltpu
from jax.sharding import Mesh, PartitionSpec as P

BF16 = jnp.bfloat16
F32 = jnp.float32
AXES = ("x", "yl", "yh", "z", "core")
SIZES = (4, 2, 4, 8, 2)
NX, NL, NH, NZ, NC = SIZES


def place(y):
    return (y % NL) * NH + y // NL


def intra(block):
    return lax.ppermute(block, "yl", [(0, 1), (1, 0)])


def inter(block):
    ny = NL * NH
    pairs = []
    for j in range(NH):
        a, b = place(2 * j + 1), place((2 * j + 2) % ny)
        pairs += [(a, b), (b, a)]
    return lax.ppermute(block, ("yl", "yh"), pairs)


def after(value, *others):
    return lax.optimization_barrier((value, *[o[:16] for o in others]))


def dot(left, right):
    return lax.dot_general(left, right, (((1,), (1,)), ((), ())), preferred_element_type=F32)


def product_kernel(halves, unread, *refs):
    count = len(halves)
    rows_refs, pieces = refs[:2], refs[2 : 2 + 2 * count]
    out_ref, left, right, left_sem, right_sem = refs[2 + 2 * count + unread :]
    yl, core = lax.axis_index("yl"), lax.axis_index("core")
    _, nz, rows, width = rows_refs[0].shape
    part = pieces[0].shape[0]
    wide = rows // NX
    lefts = [[None, None], [None, None]]
    for which in range(2):
        for half in range(2):
            source = rows_refs[which].at[yl if half == 0 else 1 - yl]
            lefts[which][half] = pltpu.make_async_copy(
                source, left.at[which, half], left_sem.at[which, half]
            )
    rights = []
    for i in range(count):
        for p in range(2):
            rights.append(
                pltpu.make_async_copy(
                    pieces[2 * i + p], right.at[i, pl.ds(p * part, part)], right_sem.at[i, p]
                )
            )
    first = halves[0]
    lefts[0][first].start()
    rights[0].start()
    rights[1].start()
    lefts[0][1 - first].start()
    for copy in rights[2:4]:
        copy.start()
    lefts[1][first].start()
    lefts[1][1 - first].start()
    for copy in rights[4:]:
        copy.start()
    for which in range(2):
        target_core = core if which == 0 else 1 - core
        done = []
        for slot in range(count // 2):
            total = None
            for i in (2 * slot, 2 * slot + 1):
                if which == 0:
                    rights[2 * i].wait()
                    rights[2 * i + 1].wait()
                if slot == 0:
                    lefts[which][halves[i]].wait()
                term = dot(left[which, halves[i]].reshape(nz * rows, width), right[i])
                total = term if total is None else total + term
            done.append(total)
        for zi in range(nz):
            for xi in range(NX):
                at = zi * rows + xi * wide
                block = jnp.concatenate([d[at : at + wide] for d in done], axis=0)
                out_ref[(xi * nz + zi) * NC + target_core] = block.astype(BF16)


def product(mine, other, blocks, halves, unread):
    _, nz, rows, width = mine.shape
    wide = rows // NX
    columns = 2 * blocks[0][0].shape[0]
    count = len(blocks)
    members = NX * nz * NC
    flops = 2 * 2 * nz * rows * width * columns * count
    anywhere = pl.BlockSpec(memory_space=pltpu.HBM)
    return pl.pallas_call(
        functools.partial(product_kernel, halves, len(unread)),
        out_shape=jax.ShapeDtypeStruct((members, count // 2 * wide, columns), BF16),
        in_specs=[anywhere] * (2 + 2 * count + len(unread)),
        out_specs=pl.BlockSpec(memory_space=pltpu.VMEM),
        scratch_shapes=[
            pltpu.VMEM((2, 2, nz, rows, width), BF16),
            pltpu.VMEM((count, columns, width), BF16),
            pltpu.SemaphoreType.DMA((2, 2)),
            pltpu.SemaphoreType.DMA((count, 2)),
        ],
        compiler_params=pltpu.CompilerParams(vmem_limit_bytes=60 * 1024 * 1024),
        cost_estimate=pl.CostEstimate(flops=flops, bytes_accessed=5 * 2**20, transcendentals=0),
    )(mine, other, *[piece for block in blocks for piece in block], *unread)


def finish_kernel(terms_ref, out_ref):
    yh = lax.axis_index("yh")
    step = 1 - 2 * lax.axis_index("yl")
    total = terms_ref[0].astype(F32)
    for xi in range(1, NX):
        total = total + terms_ref[xi].astype(F32)
    wide = total.shape[1] // NH
    for slot, offset in enumerate((0, -step, step, 2)):
        out_ref[lax.rem(yh + NH + offset, NH)] = total[:, slot * wide : (slot + 1) * wide]


def finish(terms):
    members, tall, columns = terms.shape
    rest = members // NX
    terms = terms.reshape(NX, rest, tall, columns)
    step = rest // 2
    return pl.pallas_call(
        finish_kernel,
        grid=(rest // step,),
        out_shape=jax.ShapeDtypeStruct((NH, rest, tall // NH, columns), F32),
        in_specs=[pl.BlockSpec((NX, step, tall, columns), lambda i: (0, i, 0, 0))],
        out_specs=pl.BlockSpec((NH, step, tall // NH, columns), lambda i: (0, i, 0, 0)),
        cost_estimate=pl.CostEstimate(flops=2**19, bytes_accessed=3 * 2**19, transcendentals=0),
    )(terms)


def body(valence_pairs, conduction_pairs, screening):
    _, second, plane_dev = valence_pairs.shape
    own = conduction_pairs[0]
    cut = own.shape[0] // 2
    own_a, own_b = own[:cut], own[cut:]

    f1a, b1a = intra(own_a), inter(own_a)
    f1b, b1b = intra(own_b), inter(own_b)

    screened = (valence_pairs[0].astype(F32) * screening[None, :]).astype(BF16)
    wide = second // (NX * NL)
    by_half = screened.reshape(NX, NL, wide, plane_dev).transpose(1, 0, 2, 3)
    by_half = by_half.reshape(NL, 1, NX * wide, plane_dev)
    sent = jnp.broadcast_to(by_half, (NL, NZ, NX * wide, plane_dev))
    sent = sent.reshape(NL * NZ, NX * wide, plane_dev)
    mine = lax.all_to_all(sent, ("yl", "z"), 0, 0, tiled=True)

    f2a, b2a = intra(b1a), inter(f1a)
    f2b, b2b = intra(b1b), inter(f1b)
    f3a, b3a = intra(b2a), inter(f2a)
    f3b, b3b = intra(b2b), inter(f2b)
    f4a, b4b = intra(b3a), inter(f3b)

    mine, *rows = after(mine, f3a, b3a, f3b, b3b)
    other = lax.ppermute(mine, "core", [(0, 1), (1, 0)])
    mine = mine.reshape(NL, NZ, NX * wide, plane_dev)
    other = other.reshape(NL, NZ, NX * wide, plane_dev)

    terms = product(
        mine,
        other,
        (
            (own_a, own_b), (f1a, f1b), (b1a, b1b), (b2a, b2b),
            (f2a, f2b), (f3a, f3b), (b3a, b3b), (f4a, b4b),
        ),
        (0, 1, 1, 0, 0, 1, 1, 0),
        rows,
    )
    terms = lax.all_to_all(terms, ("x", "z", "core"), 0, 0, tiled=True)
    out = finish(terms)
    return out.reshape(1, NH * NZ * NC, wide, own.shape[0])


def solution(mesh):
    fine = Mesh(mesh.devices.reshape(SIZES), AXES)
    pair, pw = ("yh", "z", "core"), ("x", "yl")
    placed = (P(pair, None, pw), P(pair, None, pw), P(pw))
    return jax.shard_map(
        body, mesh=fine, in_specs=placed, out_specs=P(pair, None, pw, None), check_vma=False
    )
```

```python
import functools

import jax
import jax.numpy as jnp
from jax import lax
from jax.experimental import pallas as pl
from jax.experimental.pallas import tpu as pltpu
from jax.sharding import Mesh, PartitionSpec as P

BF16 = jnp.bfloat16
F32 = jnp.float32
AXES = ("x", "yl", "yh", "z", "core")
SIZES = (4, 2, 4, 8, 2)
NX, NL, NH, NZ, NC = SIZES
NQ = NX * NL
LANES = 128
MIB = 2**20


def along(block, step):
    return lax.ppermute(block, "yh", [(i, (i + step) % NH) for i in range(NH)])


def dot(left, right):
    return lax.dot_general(left, right, (((1,), (1,)), ((), ())), preferred_element_type=F32)


def product_kernel(cuts, unread, begun, at_row, *refs):
    count, pieces = len(cuts), sum(cuts)
    rows_refs, piece_refs = refs[:2], refs[2 : 2 + pieces]
    out_ref, left, right, held, left_sem, right_sem, out_sem = refs[2 + pieces + unread + begun :]
    core = lax.axis_index("core")
    nz, rows, width = rows_refs[0].shape
    wide = rows // NQ
    lefts = [
        pltpu.make_async_copy(rows_refs[i], left.at[i], left_sem.at[i]) for i in range(2)
    ]
    rights, at = [], 0
    for i, cut in enumerate(cuts):
        group = []
        part = right.shape[1] // cut
        for p in range(cut):
            group.append(
                pltpu.make_async_copy(
                    piece_refs[at], right.at[i, pl.ds(p * part, part)], right_sem.at[at]
                )
            )
            at += 1
        rights.append(group)
    lefts[0].start()
    for copy in rights[0]:
        copy.start()
    lefts[1].start()
    for group in rights[1:]:
        for copy in group:
            copy.start()
    for which in range(2):
        lefts[which].wait()
        target_core = core if which == 0 else 1 - core
        whole = left[which].reshape(nz * rows, width)
        done = []
        for i in range(count):
            if which == 0:
                for copy in rights[i]:
                    copy.wait()
            term = dot(whole, right[i])
            done += [term[:, c : c + LANES] for c in range(0, term.shape[1], LANES)]
        for zi in range(nz):
            for qi in range(NQ):
                at = zi * rows + qi * wide
                block = jnp.concatenate([d[at : at + wide] for d in done], axis=0)
                held[qi, zi * NC + target_core] = block.astype(BF16)
    tall = held.shape[2]
    copy = pltpu.make_async_copy(held, out_ref.at[:, :, pl.ds(at_row, tall)], out_sem)
    copy.start()
    copy.wait()


def product(mine, other, blocks, at_row, height, unread=(), begun=None):
    nz, rows, width = mine.shape
    wide = rows // NQ
    cuts = tuple(len(block) for block in blocks)
    columns = cuts[0] * blocks[0][0].shape[0]
    count = len(blocks)
    tall = count * columns // LANES * wide
    flops = 2 * 2 * nz * rows * width * columns * count
    anywhere = pl.BlockSpec(memory_space=pltpu.HBM)
    operands = [mine, other, *[piece for block in blocks for piece in block], *unread]
    aliases = {}
    if begun is not None:
        aliases = {len(operands): 0}
        operands.append(begun)
    return pl.pallas_call(
        functools.partial(product_kernel, cuts, len(unread), len(aliases), at_row),
        out_shape=jax.ShapeDtypeStruct((NQ, nz * NC, height, LANES), BF16),
        in_specs=[anywhere] * len(operands),
        out_specs=anywhere,
        scratch_shapes=[
            pltpu.VMEM((2, nz, rows, width), BF16),
            pltpu.VMEM((count, columns, width), BF16),
            pltpu.VMEM((NQ, nz * NC, tall, LANES), BF16),
            pltpu.SemaphoreType.DMA((2,)),
            pltpu.SemaphoreType.DMA((sum(cuts),)),
            pltpu.SemaphoreType.DMA,
        ],
        input_output_aliases=aliases,
        compiler_params=pltpu.CompilerParams(vmem_limit_bytes=40 * MIB),
        cost_estimate=pl.CostEstimate(flops=flops, bytes_accessed=5 * MIB, transcendentals=0),
    )(*operands)


def add_kernel(*refs):
    out_ref, at = refs[-1], 0
    for ref in refs[:-1]:
        total = ref[0].astype(F32)
        for qi in range(1, NQ):
            total = total + ref[qi].astype(F32)
        tall = total.shape[1]
        out_ref[:, at : at + tall] = total.astype(BF16)
        at += tall


def add(*terms):
    rest = terms[0].shape[1]
    tall = sum(t.shape[2] for t in terms)
    step = rest // 4
    return pl.pallas_call(
        add_kernel,
        grid=(rest // step,),
        out_shape=jax.ShapeDtypeStruct((rest, tall, LANES), BF16),
        in_specs=[
            pl.BlockSpec((NQ, step, t.shape[2], LANES), lambda i: (0, i, 0, 0)) for t in terms
        ],
        out_specs=pl.BlockSpec((step, tall, LANES), lambda i: (i, 0, 0)),
        cost_estimate=pl.CostEstimate(flops=MIB, bytes_accessed=2 * MIB, transcendentals=0),
    )(*terms)


def finish_kernel(terms_ref, out_ref):
    yh = lax.axis_index("yh")
    wide, columns = out_ref.shape[2:]
    values = terms_ref[...].astype(F32)
    at = 0
    for offset in (0, NH - 1, 1, 2):
        owner = lax.rem(yh + offset, NH)
        for c in range(0, columns, LANES):
            out_ref[owner, :, :, c : c + LANES] = values[:, at : at + wide]
            at += wide


def finish(terms, columns):
    rest, tall, _ = terms.shape
    wide = tall * LANES // columns // NH
    step = rest // 2
    return pl.pallas_call(
        finish_kernel,
        grid=(rest // step,),
        out_shape=jax.ShapeDtypeStruct((NH, rest, wide, columns), F32),
        in_specs=[pl.BlockSpec((step, tall, LANES), lambda i: (i, 0, 0))],
        out_specs=pl.BlockSpec((NH, step, wide, columns), lambda i: (0, i, 0, 0)),
        cost_estimate=pl.CostEstimate(flops=2**17, bytes_accessed=MIB, transcendentals=0),
    )(terms)


def body(valence_pairs, conduction_pairs, screening):
    _, second, plane_dev = valence_pairs.shape
    own = conduction_pairs[0]
    columns = own.shape[0]
    cut = columns // 2

    ahead, back = along(own, 1), along(own, NH - 1)

    screened = (valence_pairs[0].astype(F32) * screening[None, :]).astype(BF16)
    sent = jnp.broadcast_to(screened[None], (NZ, second, plane_dev))
    mine = lax.all_to_all(sent, "z", 0, 0, tiled=True)
    mine, *rows = lax.optimization_barrier((mine, ahead[:16], back[:16]))
    other = lax.ppermute(mine, "core", [(0, 1), (1, 0)])

    far = along(ahead[:cut], 1), along(back[cut:], NH - 1)

    height = NH * columns // LANES * (second // NQ)
    most = (NH - 1) * columns // LANES * (second // NQ)
    terms = product(mine, other, ((own,), (ahead,), (back,)), 0, height, rows)
    terms = product(mine, other, (far,), most, height, (), terms)
    terms = lax.all_to_all(terms, ("x", "yl"), 0, 0, tiled=True)
    terms = lax.all_to_all(add(terms), ("z", "core"), 0, 0, tiled=True)
    out = finish(terms, columns)
    return out.reshape(1, NH * NZ * NC, second // NQ, columns)


def solution(mesh):
    fine = Mesh(mesh.devices.reshape(SIZES), AXES)
    pair, pw = ("yh", "z", "core"), ("x", "yl")
    placed = (P(pair, None, pw), P(pair, None, pw), P(pw))
    return jax.shard_map(
        body, mesh=fine, in_specs=placed, out_specs=P(pair, None, pw, None), check_vma=False
    )
```

```python
import functools

import jax
import jax.numpy as jnp
from jax import lax
from jax.experimental import pallas as pl
from jax.experimental.pallas import tpu as pltpu
from jax.sharding import Mesh, PartitionSpec as P

BF16 = jnp.bfloat16
F32 = jnp.float32
AXES = ("x", "yl", "yh", "z", "core")
SIZES = (4, 2, 4, 8, 2)
NX, NL, NH, NZ, NC = SIZES
NY = NL * NH
LANES = 128
MIB = 2**20

OWN, R1, L1, R2, L2, R3, L3, FAR = range(8)
SLOTS = (
    ((OWN, OWN, 0), (L1, R1, 1)),
    ((R2, L2, 0), (R1, L1, 1)),
    ((L2, R2, 0), (L3, R3, 1)),
    ((FAR, FAR, 0), (R3, L3, 1)),
)


def place(y):
    return (y % NL) * NH + (y % NY) // NL


def around(block, step):
    pairs = [(place(y), place(y + step + NY)) for y in range(NY)]
    return lax.ppermute(block, ("yl", "yh"), pairs)


def dot(left, right):
    return lax.dot_general(left, right, (((1,), (1,)), ((), ())), preferred_element_type=F32)


def product_kernel(names, slots, ignored, at_row, *refs):
    count = len(names)
    rows_refs, piece_refs = refs[:2], refs[2 : 2 + count]
    out_ref, left, right, held, left_sem, right_sem, out_sem = refs[2 + count + ignored :]
    yl, core = lax.axis_index("yl"), lax.axis_index("core")
    nz, _, rows, width = rows_refs[0].shape
    wide = rows // NX
    blocks = []
    for name, _ in names:
        if name not in blocks:
            blocks.append(name)
    lefts = [
        [
            pltpu.make_async_copy(rows_refs[i].at[:, h], left.at[h, i], left_sem.at[h, i])
            for i in range(2)
        ]
        for h in range(2)
    ]
    rights = {name: [] for name in blocks}
    for n, (name, piece) in enumerate(names):
        target = right.at[blocks.index(name)]
        if piece is not None:
            part = right.shape[1] // 2
            target = target.at[pl.ds(piece * part, part)]
        rights[name].append(pltpu.make_async_copy(piece_refs[n], target, right_sem.at[n]))
    order = []
    for slot in slots:
        for even, odd, half in slot:
            order.append(("left", half))
            order += [("right", name) for name in {even: 0, odd: 0}]
    waits = []
    for step in order:
        if step not in waits:
            waits.append(step)
    copies = {
        step: lefts[step[1]] if step[0] == "left" else rights[step[1]] for step in waits
    }
    for step in waits:
        for copy in copies[step]:
            copy.start()
    done = []
    for slot in slots:
        total = None
        for even, odd, half in slot:
            for step in [("left", half)] + [("right", name) for name in {even: 0, odd: 0}]:
                for copy in copies.pop(step, ()):
                    copy.wait()
            where = blocks.index(even)
            if even != odd:
                where = jnp.where(yl == 0, where, blocks.index(odd))
            term = dot(left[half].reshape(2 * nz * rows, width), right[where])
            total = term if total is None else total + term
        done += [total[:, c : c + LANES] for c in range(0, total.shape[1], LANES)]
    for which in range(2):
        target_core = core if which == 0 else 1 - core
        for zi in range(nz):
            for xi in range(NX):
                at = (which * nz + zi) * rows + xi * wide
                block = jnp.concatenate([d[at : at + wide] for d in done], axis=0)
                held[(xi * nz + zi) * NC + target_core] = block.astype(BF16)
    copy = pltpu.make_async_copy(held, out_ref.at[:, pl.ds(at_row, held.shape[1])], out_sem)
    copy.start()
    copy.wait()


def product(mine, other, pieces, slots, at_row, height, unread=(), begun=None):
    nz, _, rows, width = mine.shape
    wide = rows // NX
    names = tuple(piece[:2] for piece in pieces)
    columns = 2 * pieces[-1][2].shape[0]
    if pieces[-1][1] is None:
        columns = pieces[-1][2].shape[0]
    tall = len(slots) * columns // LANES * wide
    members = NX * nz * NC
    flops = 2 * 2 * nz * rows * width * columns * 2 * len(slots)
    anywhere = pl.BlockSpec(memory_space=pltpu.HBM)
    operands = [mine, other, *[piece[2] for piece in pieces], *unread]
    ignored, aliases = len(unread), {}
    if begun is not None:
        aliases = {len(operands): 0}
        operands.append(begun)
        ignored += 1
    return pl.pallas_call(
        functools.partial(product_kernel, names, slots, ignored, at_row),
        out_shape=jax.ShapeDtypeStruct((members, height, LANES), BF16),
        in_specs=[anywhere] * len(operands),
        out_specs=anywhere,
        scratch_shapes=[
            pltpu.VMEM((2, 2, nz, rows, width), BF16),
            pltpu.VMEM((len({n for n, _ in names}), columns, width), BF16),
            pltpu.VMEM((members, tall, LANES), BF16),
            pltpu.SemaphoreType.DMA((2, 2)),
            pltpu.SemaphoreType.DMA((len(names),)),
            pltpu.SemaphoreType.DMA,
        ],
        input_output_aliases=aliases,
        compiler_params=pltpu.CompilerParams(vmem_limit_bytes=40 * MIB),
        cost_estimate=pl.CostEstimate(flops=flops, bytes_accessed=5 * MIB, transcendentals=0),
    )(*operands)


def finish_kernel(terms_ref, out_ref):
    yh = lax.axis_index("yh")
    step = 1 - 2 * lax.axis_index("yl")
    wide, columns = out_ref.shape[2:]
    total = terms_ref[0].astype(F32)
    for xi in range(1, NX):
        total = total + terms_ref[xi].astype(F32)
    at = 0
    for offset in (0, -step, step, 2):
        owner = lax.rem(yh + NH + offset, NH)
        for c in range(0, columns, LANES):
            out_ref[owner, :, :, c : c + LANES] = total[:, at : at + wide]
            at += wide


def finish(terms, columns):
    members, tall, _ = terms.shape
    rest = members // NX
    wide = tall * LANES // columns // NH
    terms = terms.reshape(NX, rest, tall, LANES)
    step = rest // 2
    return pl.pallas_call(
        finish_kernel,
        grid=(rest // step,),
        out_shape=jax.ShapeDtypeStruct((NH, rest, wide, columns), F32),
        in_specs=[pl.BlockSpec((NX, step, tall, LANES), lambda i: (0, i, 0, 0))],
        out_specs=pl.BlockSpec((NH, step, wide, columns), lambda i: (0, i, 0, 0)),
        cost_estimate=pl.CostEstimate(flops=2**19, bytes_accessed=3 * 2**19, transcendentals=0),
    )(terms)


def body(valence_pairs, conduction_pairs, screening):
    yl = lax.axis_index("yl")
    _, second, plane_dev = valence_pairs.shape
    own = conduction_pairs[0]
    columns = own.shape[0]
    cut = columns // 2
    wide = second // (NX * NL)

    screened = (valence_pairs[0].astype(F32) * screening[None, :]).astype(BF16)
    screened = screened.reshape(NX, NL, wide, plane_dev)
    kept = jnp.where(yl == 0, screened[:, 0], screened[:, 1]).reshape(NX * wide, plane_dev)
    given = jnp.where(yl == 0, screened[:, 1], screened[:, 0]).reshape(NX * wide, plane_dev)
    taken = lax.ppermute(given, "yl", [(0, 1), (1, 0)])
    r1, l1 = around(own, 1), around(own, -1)
    sent = jnp.broadcast_to(jnp.stack([kept, taken]), (NZ, NL, NX * wide, plane_dev))
    sent, *rows = lax.optimization_barrier((sent, r1[:16], l1[:16]))
    mine = lax.all_to_all(sent, "z", 0, 0, tiled=True)

    r2, l2 = around(r1, 1), around(l1, -1)
    r3, l3 = around(r2, 1), around(l2, -1)
    far = around(r3[:cut], 1), around(l3[cut:], -1)

    mine, *more = lax.optimization_barrier((mine, r3[:16], l3[:16]))
    other = lax.ppermute(mine, "core", [(0, 1), (1, 0)])

    per_slot = columns // LANES * wide
    height = len(SLOTS) * per_slot
    near = ((OWN, own), (R1, r1), (L1, l1), (R2, r2), (L2, l2), (R3, r3), (L3, l3))
    terms = product(
        mine, other, [(n, None, b) for n, b in near], SLOTS[:3], 0, height, rows + more
    )
    terms = product(
        mine, other,
        [(R3, None, r3), (L3, None, l3), (FAR, 0, far[0]), (FAR, 1, far[1])],
        SLOTS[3:], 3 * per_slot, height, (), terms,
    )
    terms = lax.all_to_all(terms, ("x", "z", "core"), 0, 0, tiled=True)
    out = finish(terms, columns)
    return out.reshape(1, NH * NZ * NC, wide, columns)


def solution(mesh):
    fine = Mesh(mesh.devices.reshape(SIZES), AXES)
    pair, pw = ("yh", "z", "core"), ("x", "yl")
    placed = (P(pair, None, pw), P(pair, None, pw), P(pw))
    return jax.shard_map(
        body, mesh=fine, in_specs=placed, out_specs=P(pair, None, pw, None), check_vma=False
    )
```

```python
import functools

import jax
import jax.numpy as jnp
from jax import lax
from jax.experimental import pallas as pl
from jax.experimental.pallas import tpu as pltpu
from jax.sharding import Mesh, PartitionSpec as P

BF16 = jnp.bfloat16
F32 = jnp.float32
AXES = ("x", "yl", "yh", "z", "core")
SIZES = (4, 2, 4, 8, 2)
NX, NL, NH, NZ, NC = SIZES
LANES = 128
MIB = 2**20

def dot(left, right):
    return lax.dot_general(left, right, (((1,), (1,)), ((), ())), preferred_element_type=F32)


def product_kernel(first, rows_ref, swapped_ref, blocks_ref, out_ref, left, right, left_sem, right_sem):
    yl, core = lax.axis_index("yl"), lax.axis_index("core")
    nz, _, rows, width = rows_ref.shape
    wide = rows // NX
    count = right.shape[0]
    lefts = [
        [
            pltpu.make_async_copy(ref.at[:, h], left.at[h, i], left_sem.at[h, i])
            for i, ref in enumerate((rows_ref, swapped_ref))
        ]
        for h in range(NL)
    ]
    rights = [
        pltpu.make_async_copy(blocks_ref.at[first * NL + n], right.at[n], right_sem.at[n])
        for n in range(count)
    ]
    for copy in [*lefts[0], rights[0], *lefts[1], *rights[1:]]:
        copy.start()
    for copy in [*lefts[0], *lefts[1]]:
        copy.wait()
    done = []
    for n in range(0, count, NL):
        total = None
        for half in range(NL):
            rights[n + half].wait()
            known = left[jnp.where(yl == half, 0, 1)].reshape(2 * nz * rows, width)
            term = dot(known, right[n + half])
            total = term if total is None else total + term
        done += [total[:, c : c + LANES] for c in range(0, total.shape[1], LANES)]
    for which in range(NC):
        target_core = core if which == 0 else 1 - core
        for zi in range(nz):
            for xi in range(NX):
                at = (which * nz + zi) * rows + xi * wide
                block = jnp.concatenate([d[at : at + wide] for d in done], axis=0)
                out_ref[(xi * nz + zi) * NC + target_core] = block.astype(BF16)


def product(mine, other, blocks, first, slots):
    nz, _, rows, width = mine.shape
    columns = blocks.shape[1]
    tall = slots * columns // LANES * rows // NX
    members = NX * nz * NC
    flops = 2 * 2 * nz * rows * width * columns * NL * slots
    anywhere = pl.BlockSpec(memory_space=pltpu.HBM)
    return pl.pallas_call(
        functools.partial(product_kernel, first),
        out_shape=jax.ShapeDtypeStruct((members, tall, LANES), BF16),
        in_specs=[anywhere] * 3,
        out_specs=pl.BlockSpec(memory_space=pltpu.VMEM),
        scratch_shapes=[
            pltpu.VMEM((NL, NC, nz, rows, width), BF16),
            pltpu.VMEM((NL * slots, columns, width), BF16),
            pltpu.SemaphoreType.DMA((NL, NC)),
            pltpu.SemaphoreType.DMA((NL * slots,)),
        ],
        compiler_params=pltpu.CompilerParams(vmem_limit_bytes=50 * MIB),
        cost_estimate=pl.CostEstimate(flops=flops, bytes_accessed=5 * MIB, transcendentals=0),
    )(mine, other, blocks)


def finish_kernel(*refs):
    out_ref, owner = refs[-1], 0
    wide, columns = out_ref.shape[2:]
    for ref in refs[:-1]:
        total = ref[0].astype(F32)
        for xi in range(1, NX):
            total = total + ref[xi].astype(F32)
        at = 0
        while at < total.shape[1]:
            for c in range(0, columns, LANES):
                out_ref[owner, :, :, c : c + LANES] = total[:, at : at + wide]
                at += wide
            owner += 1


def finish(terms, columns, wide):
    rest = terms[0].shape[0] // NX
    terms = [t.reshape(NX, rest, *t.shape[1:]) for t in terms]
    step = rest // 2
    return pl.pallas_call(
        finish_kernel,
        grid=(rest // step,),
        out_shape=jax.ShapeDtypeStruct((NH, rest, wide, columns), F32),
        in_specs=[
            pl.BlockSpec((NX, step, *t.shape[2:]), lambda i: (0, i, 0, 0)) for t in terms
        ],
        out_specs=pl.BlockSpec((NH, step, wide, columns), lambda i: (0, i, 0, 0)),
        cost_estimate=pl.CostEstimate(flops=2**19, bytes_accessed=3 * 2**19, transcendentals=0),
    )(*terms)


def body(valence_pairs, conduction_pairs, screening):
    yl = lax.axis_index("yl")
    _, second, plane_dev = valence_pairs.shape
    own = conduction_pairs[0]
    columns = own.shape[0]
    wide = second // (NX * NL)

    screened = (valence_pairs[0].astype(F32) * screening[None, :]).astype(BF16)
    screened = screened.reshape(NX, NL, wide, plane_dev)
    kept = jnp.where(yl == 0, screened[:, 0], screened[:, 1]).reshape(NX * wide, plane_dev)
    given = jnp.where(yl == 0, screened[:, 1], screened[:, 0]).reshape(NX * wide, plane_dev)
    taken = lax.ppermute(given, "yl", [(0, 1), (1, 0)])
    sent = jnp.broadcast_to(jnp.stack([kept, taken]), (NZ, NL, NX * wide, plane_dev))
    mine = lax.all_to_all(sent, "z", 0, 0, tiled=True)

    other = lax.ppermute(mine, "core", [(0, 1), (1, 0)])
    blocks = lax.all_gather(own, ("yh", "yl"), axis=0, tiled=False)

    terms = product(mine, other, blocks, 0, NH)
    terms = lax.all_to_all(terms, ("x", "z", "core"), 0, 0, tiled=True)
    out = finish([terms], columns, wide)
    return out.reshape(1, NH * NZ * NC, wide, columns)


def solution(mesh):
    fine = Mesh(mesh.devices.reshape(SIZES), AXES)
    pair, pw = ("yh", "z", "core"), ("x", "yl")
    placed = (P(pair, None, pw), P(pair, None, pw), P(pw))
    return jax.shard_map(
        body, mesh=fine, in_specs=placed, out_specs=P(pair, None, pw, None), check_vma=False
    )
```

```python
import functools

import jax
import jax.numpy as jnp
from jax import lax
from jax.experimental import pallas as pl
from jax.experimental.pallas import tpu as pltpu
from jax.sharding import Mesh, PartitionSpec as P

BF16 = jnp.bfloat16
F32 = jnp.float32
AXES = ("x", "yl", "yh", "z", "core")
SIZES = (4, 2, 4, 8, 2)
NX, NL, NH, NZ, NC = SIZES
NY = NL * NH
LANES = 128
MIB = 2**20

OWN, R1, L1, R2, L2, R3, L3, FAR = range(8)
SLOTS = (
    ((OWN, OWN, 0), (L1, R1, 1)),
    ((R2, L2, 0), (R1, L1, 1)),
    ((L2, R2, 0), (L3, R3, 1)),
    ((FAR, FAR, 0), (R3, L3, 1)),
)


def place(y):
    return (y % NL) * NH + (y % NY) // NL


def around(block, step):
    pairs = [(place(y), place(y + step + NY)) for y in range(NY)]
    return lax.ppermute(block, ("yl", "yh"), pairs)


def dot(left, right):
    return lax.dot_general(left, right, (((1,), (1,)), ((), ())), preferred_element_type=F32)


def product_kernel(names, slots, ignored, at_row, *refs):
    count = len(names)
    rows_ref, piece_refs = refs[0], refs[1 : 1 + count]
    out_ref, left, right, held, left_sem, right_sem, out_sem = refs[1 + count + ignored :]
    yl = lax.axis_index("yl")
    nz, _, rows, width = rows_ref.shape
    wide = rows // NX
    blocks = []
    for name, _ in names:
        if name not in blocks:
            blocks.append(name)
    lefts = [
        [pltpu.make_async_copy(rows_ref.at[:, h], left.at[h], left_sem.at[h])] for h in range(2)
    ]
    rights = {name: [] for name in blocks}
    for n, (name, piece) in enumerate(names):
        target = right.at[blocks.index(name)]
        if piece is not None:
            part = right.shape[1] // 2
            target = target.at[pl.ds(piece * part, part)]
        rights[name].append(pltpu.make_async_copy(piece_refs[n], target, right_sem.at[n]))
    order = []
    for slot in slots:
        for even, odd, half in slot:
            order.append(("left", half))
            order += [("right", name) for name in {even: 0, odd: 0}]
    waits = []
    for step in order:
        if step not in waits:
            waits.append(step)
    copies = {
        step: lefts[step[1]] if step[0] == "left" else rights[step[1]] for step in waits
    }
    for step in waits:
        for copy in copies[step]:
            copy.start()
    done = []
    for slot in slots:
        total = None
        for even, odd, half in slot:
            for step in [("left", half)] + [("right", name) for name in {even: 0, odd: 0}]:
                for copy in copies.pop(step, ()):
                    copy.wait()
            where = blocks.index(even)
            if even != odd:
                where = jnp.where(yl == 0, where, blocks.index(odd))
            term = dot(left[half].reshape(nz * rows, width), right[where])
            total = term if total is None else total + term
        done += [total[:, c : c + LANES] for c in range(0, total.shape[1], LANES)]
    for owner in range(nz):
        for xi in range(NX):
            at = owner * rows + xi * wide
            block = jnp.concatenate([d[at : at + wide] for d in done], axis=0)
            held[xi * nz + owner] = block.astype(BF16)
    copy = pltpu.make_async_copy(held, out_ref.at[:, pl.ds(at_row, held.shape[1])], out_sem)
    copy.start()
    copy.wait()


def product(mine, pieces, slots, at_row, height, unread=(), begun=None):
    nz, _, rows, width = mine.shape
    wide = rows // NX
    names = tuple(piece[:2] for piece in pieces)
    columns = 2 * pieces[-1][2].shape[0]
    if pieces[-1][1] is None:
        columns = pieces[-1][2].shape[0]
    tall = len(slots) * columns // LANES * wide
    members = NX * nz
    flops = 2 * nz * rows * width * columns * 2 * len(slots)
    anywhere = pl.BlockSpec(memory_space=pltpu.HBM)
    operands = [mine, *[piece[2] for piece in pieces], *unread]
    ignored, aliases = len(unread), {}
    if begun is not None:
        aliases = {len(operands): 0}
        operands.append(begun)
        ignored += 1
    return pl.pallas_call(
        functools.partial(product_kernel, names, slots, ignored, at_row),
        out_shape=jax.ShapeDtypeStruct((members, height, LANES), BF16),
        in_specs=[anywhere] * len(operands),
        out_specs=anywhere,
        scratch_shapes=[
            pltpu.VMEM((2, nz, rows, width), BF16),
            pltpu.VMEM((len({n for n, _ in names}), columns, width), BF16),
            pltpu.VMEM((members, tall, LANES), BF16),
            pltpu.SemaphoreType.DMA((2,)),
            pltpu.SemaphoreType.DMA((len(names),)),
            pltpu.SemaphoreType.DMA,
        ],
        input_output_aliases=aliases,
        compiler_params=pltpu.CompilerParams(vmem_limit_bytes=60 * MIB),
        cost_estimate=pl.CostEstimate(flops=flops, bytes_accessed=5 * MIB, transcendentals=0),
    )(*operands)


def finish_kernel(terms_ref, out_ref):
    yh = lax.axis_index("yh")
    step = 1 - 2 * lax.axis_index("yl")
    wide, columns = out_ref.shape[2:]
    total = terms_ref[0].astype(F32)
    for xi in range(1, NX):
        total = total + terms_ref[xi].astype(F32)
    at = 0
    for offset in (0, -step, step, 2):
        owner = lax.rem(yh + NH + offset, NH)
        for c in range(0, columns, LANES):
            out_ref[owner, :, :, c : c + LANES] = total[:, at : at + wide]
            at += wide


def finish(terms, columns):
    members, tall, _ = terms.shape
    rest = members // NX
    wide = tall * LANES // columns // NH
    terms = terms.reshape(NX, rest, tall, LANES)
    step = rest // 2
    return pl.pallas_call(
        finish_kernel,
        grid=(rest // step,),
        out_shape=jax.ShapeDtypeStruct((NH, rest, wide, columns), F32),
        in_specs=[pl.BlockSpec((NX, step, tall, LANES), lambda i: (0, i, 0, 0))],
        out_specs=pl.BlockSpec((NH, step, wide, columns), lambda i: (0, i, 0, 0)),
        cost_estimate=pl.CostEstimate(flops=2**19, bytes_accessed=3 * 2**19, transcendentals=0),
    )(terms)


def body(valence_pairs, conduction_pairs, screening):
    yl = lax.axis_index("yl")
    _, second, plane_dev = valence_pairs.shape
    own = conduction_pairs[0]
    columns = own.shape[0]
    cut = columns // 2
    wide = second // (NX * NL)

    screened = (valence_pairs[0].astype(F32) * screening[None, :]).astype(BF16)
    screened = screened.reshape(NX, NL, wide, plane_dev)
    kept = jnp.where(yl == 0, screened[:, 0], screened[:, 1]).reshape(NX * wide, plane_dev)
    given = jnp.where(yl == 0, screened[:, 1], screened[:, 0]).reshape(NX * wide, plane_dev)
    taken = lax.ppermute(given, "yl", [(0, 1), (1, 0)])
    r1, l1 = around(own, 1), around(own, -1)
    sent = jnp.broadcast_to(jnp.stack([kept, taken]), (NZ * NC, NL, NX * wide, plane_dev))
    mine = lax.all_to_all(sent, ("z", "core"), 0, 0, tiled=True)

    r2, l2 = around(r1, 1), around(l1, -1)
    r3, l3 = around(r2, 1), around(l2, -1)
    far = around(r3[:cut], 1), around(l3[cut:], -1)

    per_slot = columns // LANES * wide
    height = len(SLOTS) * per_slot
    near = ((OWN, own), (R1, r1), (L1, l1), (R2, r2), (L2, l2), (R3, r3), (L3, l3))
    terms = product(
        mine, [(n, None, b) for n, b in near], SLOTS[:3], 0, height
    )
    terms = product(
        mine,
        [(R3, None, r3), (L3, None, l3), (FAR, 0, far[0]), (FAR, 1, far[1])],
        SLOTS[3:], 3 * per_slot, height, (), terms,
    )
    terms = lax.all_to_all(terms, ("x", "z", "core"), 0, 0, tiled=True)
    out = finish(terms, columns)
    return out.reshape(1, NH * NZ * NC, wide, columns)


def solution(mesh):
    fine = Mesh(mesh.devices.reshape(SIZES), AXES)
    pair, pw = ("yh", "z", "core"), ("x", "yl")
    placed = (P(pair, None, pw), P(pair, None, pw), P(pw))
    return jax.shard_map(
        body, mesh=fine, in_specs=placed, out_specs=P(pair, None, pw, None), check_vma=False
    )
```

```python
import functools

import jax
import jax.numpy as jnp
from jax import lax
from jax.experimental import pallas as pl
from jax.experimental.pallas import tpu as pltpu
from jax.sharding import Mesh, PartitionSpec as P

BF16 = jnp.bfloat16
F32 = jnp.float32
AXES = ("x", "yl", "yh", "z", "core")
SIZES = (4, 2, 4, 8, 2)
NX, NL, NH, NZ, NC = SIZES
NQ = NX * NL
LANES = 128
MIB = 2**20


def along(block, step):
    return lax.ppermute(block, "yh", [(i, (i + step) % NH) for i in range(NH)])


def dot(left, right):
    return lax.dot_general(left, right, (((1,), (1,)), ((), ())), preferred_element_type=F32)


def mark_kernel(seen_ref, out_ref):
    out_ref[...] = seen_ref[...]


def mark(seen):
    return pl.pallas_call(
        mark_kernel,
        out_shape=jax.ShapeDtypeStruct(seen.shape, seen.dtype),
        compiler_params=pltpu.CompilerParams(vmem_limit_bytes=MIB),
        cost_estimate=pl.CostEstimate(flops=10**11, bytes_accessed=10**8, transcendentals=0),
    )(seen)


def product_kernel(cuts, unread, begun, at_row, *refs):
    count, pieces = len(cuts), sum(cuts)
    rows_refs, piece_refs = refs[:2], refs[2 : 2 + pieces]
    out_ref, left, right, held, left_sem, right_sem, out_sem = refs[2 + pieces + unread + begun :]
    core = lax.axis_index("core")
    nz, rows, width = rows_refs[0].shape
    wide = rows // NQ
    lefts = [
        pltpu.make_async_copy(rows_refs[i], left.at[i], left_sem.at[i]) for i in range(2)
    ]
    rights, at = [], 0
    for i, cut in enumerate(cuts):
        group = []
        part = right.shape[1] // cut
        for p in range(cut):
            group.append(
                pltpu.make_async_copy(
                    piece_refs[at], right.at[i, pl.ds(p * part, part)], right_sem.at[at]
                )
            )
            at += 1
        rights.append(group)
    lefts[0].start()
    for copy in rights[0]:
        copy.start()
    lefts[1].start()
    for group in rights[1:]:
        for copy in group:
            copy.start()
    for which in range(2):
        lefts[which].wait()
        target_core = core if which == 0 else 1 - core
        whole = left[which].reshape(nz * rows, width)
        done = []
        for i in range(count):
            if which == 0:
                for copy in rights[i]:
                    copy.wait()
            term = dot(whole, right[i])
            done += [term[:, c : c + LANES] for c in range(0, term.shape[1], LANES)]
        for zi in range(nz):
            for qi in range(NQ):
                at = zi * rows + qi * wide
                block = jnp.concatenate([d[at : at + wide] for d in done], axis=0)
                held[qi, zi * NC + target_core] = block.astype(BF16)
    tall = held.shape[2]
    copy = pltpu.make_async_copy(held, out_ref.at[:, :, pl.ds(at_row, tall)], out_sem)
    copy.start()
    copy.wait()


def product(mine, other, blocks, at_row, height, unread=(), begun=None):
    nz, rows, width = mine.shape
    wide = rows // NQ
    cuts = tuple(len(block) for block in blocks)
    columns = cuts[0] * blocks[0][0].shape[0]
    count = len(blocks)
    tall = count * columns // LANES * wide
    flops = 2 * 2 * nz * rows * width * columns * count
    anywhere = pl.BlockSpec(memory_space=pltpu.HBM)
    operands = [mine, other, *[piece for block in blocks for piece in block], *unread]
    aliases = {}
    if begun is not None:
        aliases = {len(operands): 0}
        operands.append(begun)
    return pl.pallas_call(
        functools.partial(product_kernel, cuts, len(unread), len(aliases), at_row),
        out_shape=jax.ShapeDtypeStruct((NQ, nz * NC, height, LANES), BF16),
        in_specs=[anywhere] * len(operands),
        out_specs=pl.BlockSpec(memory_space=pl.ANY),
        scratch_shapes=[
            pltpu.VMEM((2, nz, rows, width), BF16),
            pltpu.VMEM((count, columns, width), BF16),
            pltpu.VMEM((NQ, nz * NC, tall, LANES), BF16),
            pltpu.SemaphoreType.DMA((2,)),
            pltpu.SemaphoreType.DMA((sum(cuts),)),
            pltpu.SemaphoreType.DMA,
        ],
        input_output_aliases=aliases,
        compiler_params=pltpu.CompilerParams(vmem_limit_bytes=24 * MIB),
        cost_estimate=pl.CostEstimate(flops=flops, bytes_accessed=5 * MIB, transcendentals=0),
    )(*operands)


def add_kernel(*refs):
    out_ref, at = refs[-1], 0
    for ref in refs[:-1]:
        total = ref[0].astype(F32)
        for qi in range(1, NQ):
            total = total + ref[qi].astype(F32)
        tall = total.shape[1]
        out_ref[:, at : at + tall] = total.astype(BF16)
        at += tall


def add(*terms):
    rest = terms[0].shape[1]
    tall = sum(t.shape[2] for t in terms)
    step = rest // 4
    return pl.pallas_call(
        add_kernel,
        grid=(rest // step,),
        out_shape=jax.ShapeDtypeStruct((rest, tall, LANES), BF16),
        in_specs=[
            pl.BlockSpec((NQ, step, t.shape[2], LANES), lambda i: (0, i, 0, 0)) for t in terms
        ],
        out_specs=pl.BlockSpec((step, tall, LANES), lambda i: (i, 0, 0)),
        compiler_params=pltpu.CompilerParams(vmem_limit_bytes=8 * MIB),
        cost_estimate=pl.CostEstimate(flops=MIB, bytes_accessed=2 * MIB, transcendentals=0),
    )(*terms)


def finish_kernel(terms_ref, out_ref):
    yh = lax.axis_index("yh")
    wide, columns = out_ref.shape[2:]
    values = terms_ref[...].astype(F32)
    at = 0
    for offset in (0, NH - 1, 1, 2):
        owner = lax.rem(yh + offset, NH)
        for c in range(0, columns, LANES):
            out_ref[owner, :, :, c : c + LANES] = values[:, at : at + wide]
            at += wide


def finish(terms, columns):
    rest, tall, _ = terms.shape
    wide = tall * LANES // columns // NH
    step = rest // 2
    return pl.pallas_call(
        finish_kernel,
        grid=(rest // step,),
        out_shape=jax.ShapeDtypeStruct((NH, rest, wide, columns), F32),
        in_specs=[pl.BlockSpec((step, tall, LANES), lambda i: (i, 0, 0))],
        out_specs=pl.BlockSpec((NH, step, wide, columns), lambda i: (0, i, 0, 0)),
        compiler_params=pltpu.CompilerParams(vmem_limit_bytes=8 * MIB),
        cost_estimate=pl.CostEstimate(flops=2**17, bytes_accessed=MIB, transcendentals=0),
    )(terms)


def body(valence_pairs, conduction_pairs, screening):
    _, second, plane_dev = valence_pairs.shape
    own = conduction_pairs[0]
    columns = own.shape[0]
    cut = columns // 2

    ahead, back = along(own, 1), along(own, NH - 1)

    screened = (valence_pairs[0].astype(F32) * screening[None, :]).astype(BF16)
    sent = jnp.broadcast_to(screened[None], (NZ, second, plane_dev))
    mine = lax.all_to_all(sent, "z", 0, 0, tiled=True)
    mine, *rows = lax.optimization_barrier((mine, ahead[:16], back[:16], mark(screening[None])))
    other = lax.ppermute(mine, "core", [(0, 1), (1, 0)])

    far = along(ahead[:cut], 1), along(back[cut:], NH - 1)
    other, *more = lax.optimization_barrier((other, mark(back[:16])))

    height = NH * columns // LANES * (second // NQ)
    most = (NH - 1) * columns // LANES * (second // NQ)
    terms = product(mine, other, ((own,), (ahead,), (back,)), 0, height, rows + more)
    terms = product(mine, other, (far,), most, height, (), terms)
    terms = lax.all_to_all(terms, ("x", "yl"), 0, 0, tiled=True)
    terms = lax.all_to_all(add(terms), ("z", "core"), 0, 0, tiled=True)
    out = finish(terms, columns)
    return out.reshape(1, NH * NZ * NC, second // NQ, columns)


def solution(mesh):
    fine = Mesh(mesh.devices.reshape(SIZES), AXES)
    pair, pw = ("yh", "z", "core"), ("x", "yl")
    placed = (P(pair, None, pw), P(pair, None, pw), P(pw))
    return jax.shard_map(
        body, mesh=fine, in_specs=placed, out_specs=P(pair, None, pw, None), check_vma=False
    )
```

```python
import functools

import jax
import jax.numpy as jnp
from jax import lax
from jax.experimental import pallas as pl
from jax.experimental.pallas import tpu as pltpu
from jax.sharding import Mesh, PartitionSpec as P

BF16 = jnp.bfloat16
F32 = jnp.float32
AXES = ("x", "yl", "yh", "z", "core")
SIZES = (4, 2, 4, 8, 2)
NX, NL, NH, NZ, NC = SIZES
NQ = NX * NL
LANES = 128
MIB = 2**20


def along(block, step):
    return lax.ppermute(block, "yh", [(i, (i + step) % NH) for i in range(NH)])


def dot(left, right):
    return lax.dot_general(left, right, (((1,), (1,)), ((), ())), preferred_element_type=F32)


def screen_kernel(pairs_ref, screening_ref, out_ref):
    screened = (pairs_ref[...].astype(F32) * screening_ref[...]).astype(BF16)
    for i in range(out_ref.shape[0]):
        out_ref[i] = screened


def screen(pairs, screening, copies):
    return pl.pallas_call(
        screen_kernel,
        out_shape=jax.ShapeDtypeStruct((copies, *pairs.shape), BF16),
        compiler_params=pltpu.CompilerParams(vmem_limit_bytes=4 * MIB),
        cost_estimate=pl.CostEstimate(flops=2**16, bytes_accessed=MIB, transcendentals=0),
    )(pairs, screening[None])


def mark_kernel(seen_ref, out_ref):
    out_ref[...] = seen_ref[...]


def mark(seen):
    return pl.pallas_call(
        mark_kernel,
        out_shape=jax.ShapeDtypeStruct(seen.shape, seen.dtype),
        compiler_params=pltpu.CompilerParams(vmem_limit_bytes=MIB),
        cost_estimate=pl.CostEstimate(flops=10**11, bytes_accessed=10**8, transcendentals=0),
    )(seen)


def product_kernel(cuts, unread, begun, at_row, *refs):
    count, pieces = len(cuts), sum(cuts)
    rows_refs, piece_refs = refs[:2], refs[2 : 2 + pieces]
    out_ref, left, right, held, left_sem, right_sem, out_sem = refs[2 + pieces + unread + begun :]
    core = lax.axis_index("core")
    nz, rows, width = rows_refs[0].shape
    wide = rows // NQ
    lefts = [
        pltpu.make_async_copy(rows_refs[i], left.at[i], left_sem.at[i]) for i in range(2)
    ]
    rights, at = [], 0
    for i, cut in enumerate(cuts):
        group, top = [], 0
        for _ in range(cut):
            part = piece_refs[at].shape[0]
            group.append(
                pltpu.make_async_copy(
                    piece_refs[at], right.at[i, pl.ds(top, part)], right_sem.at[at]
                )
            )
            at, top = at + 1, top + part
        rights.append(group)
    lefts[0].start()
    for copy in rights[0]:
        copy.start()
    lefts[1].start()
    for group in rights[1:]:
        for copy in group:
            copy.start()
    for copy in lefts:
        copy.wait()
    whole = left[...].reshape(2 * nz * rows, width)
    done = []
    for i in range(count):
        for copy in rights[i]:
            copy.wait()
        term = dot(whole, right[i])
        done += [term[:, c : c + LANES] for c in range(0, term.shape[1], LANES)]
    for which in range(2):
        target_core = core if which == 0 else 1 - core
        for zi in range(nz):
            for qi in range(NQ):
                at = (which * nz + zi) * rows + qi * wide
                block = jnp.concatenate([d[at : at + wide] for d in done], axis=0)
                held[qi, zi * NC + target_core] = block.astype(BF16)
    tall = held.shape[2]
    copy = pltpu.make_async_copy(held, out_ref.at[:, :, pl.ds(at_row, tall)], out_sem)
    copy.start()
    copy.wait()


def product(mine, other, blocks, at_row, height, unread=(), begun=None):
    nz, rows, width = mine.shape
    wide = rows // NQ
    cuts = tuple(len(block) for block in blocks)
    columns = sum(piece.shape[0] for piece in blocks[0])
    count = len(blocks)
    tall = count * columns // LANES * wide
    flops = 2 * 2 * nz * rows * width * columns * count
    anywhere = pl.BlockSpec(memory_space=pltpu.HBM)
    operands = [mine, other, *[piece for block in blocks for piece in block], *unread]
    aliases = {}
    if begun is not None:
        aliases = {len(operands): 0}
        operands.append(begun)
    return pl.pallas_call(
        functools.partial(product_kernel, cuts, len(unread), len(aliases), at_row),
        out_shape=jax.ShapeDtypeStruct((NQ, nz * NC, height, LANES), BF16),
        in_specs=[anywhere] * len(operands),
        out_specs=pl.BlockSpec(memory_space=pl.ANY),
        scratch_shapes=[
            pltpu.VMEM((2, nz, rows, width), BF16),
            pltpu.VMEM((count, columns, width), BF16),
            pltpu.VMEM((NQ, nz * NC, tall, LANES), BF16),
            pltpu.SemaphoreType.DMA((2,)),
            pltpu.SemaphoreType.DMA((sum(cuts),)),
            pltpu.SemaphoreType.DMA,
        ],
        input_output_aliases=aliases,
        compiler_params=pltpu.CompilerParams(vmem_limit_bytes=14 * MIB),
        cost_estimate=pl.CostEstimate(flops=flops, bytes_accessed=5 * MIB, transcendentals=0),
    )(*operands)


def add_kernel(*refs):
    out_ref, at = refs[-1], 0
    for ref in refs[:-1]:
        total = ref[0].astype(F32)
        for qi in range(1, NQ):
            total = total + ref[qi].astype(F32)
        tall = total.shape[1]
        out_ref[:, at : at + tall] = total.astype(BF16)
        at += tall


def add(*terms):
    rest = terms[0].shape[1]
    tall = sum(t.shape[2] for t in terms)
    step = rest // 4
    return pl.pallas_call(
        add_kernel,
        grid=(rest // step,),
        out_shape=jax.ShapeDtypeStruct((rest, tall, LANES), BF16),
        in_specs=[
            pl.BlockSpec((NQ, step, t.shape[2], LANES), lambda i: (0, i, 0, 0)) for t in terms
        ],
        out_specs=pl.BlockSpec((step, tall, LANES), lambda i: (i, 0, 0)),
        compiler_params=pltpu.CompilerParams(vmem_limit_bytes=8 * MIB),
        cost_estimate=pl.CostEstimate(flops=MIB, bytes_accessed=2 * MIB, transcendentals=0),
    )(*terms)


def finish_kernel(terms_ref, out_ref):
    yh = lax.axis_index("yh")
    wide, columns = out_ref.shape[2:]
    values = terms_ref[...].astype(F32)
    at = 0
    for offset in (0, NH - 1, 1, 2):
        owner = lax.rem(yh + offset, NH)
        for c in range(0, columns, LANES):
            out_ref[owner, :, :, c : c + LANES] = values[:, at : at + wide]
            at += wide


def finish(terms, columns):
    rest, tall, _ = terms.shape
    wide = tall * LANES // columns // NH
    step = rest // 2
    return pl.pallas_call(
        finish_kernel,
        grid=(rest // step,),
        out_shape=jax.ShapeDtypeStruct((NH, rest, wide, columns), F32),
        in_specs=[pl.BlockSpec((step, tall, LANES), lambda i: (i, 0, 0))],
        out_specs=pl.BlockSpec((NH, step, wide, columns), lambda i: (0, i, 0, 0)),
        compiler_params=pltpu.CompilerParams(vmem_limit_bytes=8 * MIB),
        cost_estimate=pl.CostEstimate(flops=2**17, bytes_accessed=MIB, transcendentals=0),
    )(terms)


def body(valence_pairs, conduction_pairs, screening):
    _, second, plane_dev = valence_pairs.shape
    own = conduction_pairs[0]
    columns = own.shape[0]
    cut = columns * 5 // 8

    ahead, back = along(own, 1), along(own, NH - 1)

    sent = screen(valence_pairs[0], screening, NZ)
    mine = lax.all_to_all(sent, "z", 0, 0, tiled=True)
    mine, *rows = lax.optimization_barrier((mine, ahead[:16], back[:16], mark(screening[None])))
    other = lax.ppermute(mine, "core", [(0, 1), (1, 0)])

    far = along(ahead[:cut], 1), along(back[cut:], NH - 1)
    other, *more = lax.optimization_barrier((other, mark(back[:16])))

    height = NH * columns // LANES * (second // NQ)
    most = (NH - 1) * columns // LANES * (second // NQ)
    terms = product(mine, other, ((own,), (ahead,), (back,)), 0, height, rows + more)
    terms = product(mine, other, (far,), most, height, (), terms)
    terms = lax.all_to_all(terms, ("x", "yl"), 0, 0, tiled=True)
    terms = lax.all_to_all(add(terms), ("z", "core"), 0, 0, tiled=True)
    out = finish(terms, columns)
    return out.reshape(1, NH * NZ * NC, second // NQ, columns)


def solution(mesh):
    fine = Mesh(mesh.devices.reshape(SIZES), AXES)
    pair, pw = ("yh", "z", "core"), ("x", "yl")
    placed = (P(pair, None, pw), P(pair, None, pw), P(pw))
    return jax.shard_map(
        body, mesh=fine, in_specs=placed, out_specs=P(pair, None, pw, None), check_vma=False
    )
```

```python
import functools

import jax
import jax.numpy as jnp
from jax import lax
from jax.experimental import pallas as pl
from jax.experimental.pallas import tpu as pltpu
from jax.sharding import Mesh, PartitionSpec as P

BF16 = jnp.bfloat16
F32 = jnp.float32
AXES = ("x", "yl", "yh", "z", "core")
SIZES = (4, 2, 4, 8, 2)
NX, NL, NH, NZ, NC = SIZES
NQ = NX * NL
LANES = 128
MIB = 2**20
LONG = 10**11


def along(block, step):
    return lax.ppermute(block, "yh", [(i, (i + step) % NH) for i in range(NH)])


def dot(left, right):
    return lax.dot_general(left, right, (((1,), (1,)), ((), ())), preferred_element_type=F32)


def mark_kernel(seen_ref, out_ref):
    out_ref[...] = seen_ref[...]


def mark(seen):
    return pl.pallas_call(
        mark_kernel,
        out_shape=jax.ShapeDtypeStruct(seen.shape, seen.dtype),
        compiler_params=pltpu.CompilerParams(vmem_limit_bytes=MIB),
        cost_estimate=pl.CostEstimate(flops=LONG, bytes_accessed=10**8, transcendentals=0),
    )(seen)


def product_kernel(sides, cuts, ignored, at_row, *refs):
    count, pieces, width = len(cuts), sum(cuts), len(sides)
    rows_refs, piece_refs = refs[:width], refs[width : width + pieces]
    out_ref, left, right, held, left_sem, right_sem, out_sem = refs[width + pieces + ignored :]
    core = lax.axis_index("core")
    nz, rows, planes = rows_refs[0].shape
    wide = rows // NQ
    lefts = [
        pltpu.make_async_copy(rows_refs[i], left.at[i], left_sem.at[i]) for i in range(width)
    ]
    rights, at = [], 0
    for i, cut in enumerate(cuts):
        group, top = [], 0
        for _ in range(cut):
            part = piece_refs[at].shape[0]
            group.append(
                pltpu.make_async_copy(
                    piece_refs[at], right.at[i, pl.ds(top, part)], right_sem.at[at]
                )
            )
            at, top = at + 1, top + part
        rights.append(group)
    for copy in [*lefts, *[copy for group in rights for copy in group]]:
        copy.start()
    for copy in lefts:
        copy.wait()
    whole = left[...].reshape(width * nz * rows, planes)
    done = []
    for i in range(count):
        for copy in rights[i]:
            copy.wait()
        term = dot(whole, right[i])
        done += [term[:, c : c + LANES] for c in range(0, term.shape[1], LANES)]
    tall = held.shape[3]
    copies = []
    for n, side in enumerate(sides):
        for zi in range(nz):
            for qi in range(NQ):
                at = (n * nz + zi) * rows + qi * wide
                block = jnp.concatenate([d[at : at + wide] for d in done], axis=0)
                held[n, qi, zi] = block.astype(BF16)
        owner = core if side == 0 else 1 - core
        target = out_ref.at[:, :, owner, pl.ds(at_row, tall)]
        copies.append(pltpu.make_async_copy(held.at[n], target, out_sem.at[n]))
        copies[-1].start()
    for copy in copies:
        copy.wait()


def product(lefts, sides, blocks, at_row, height, unread=(), begun=None, flops=None):
    nz, rows, width = lefts[0].shape
    wide = rows // NQ
    cuts = tuple(len(block) for block in blocks)
    columns = sum(piece.shape[0] for piece in blocks[0])
    count = len(blocks)
    tall = count * columns // LANES * wide
    if flops is None:
        flops = 2 * len(lefts) * nz * rows * width * columns * count
    anywhere = pl.BlockSpec(memory_space=pltpu.HBM)
    operands = [*lefts, *[piece for block in blocks for piece in block], *unread]
    ignored, aliases = len(unread), {}
    if begun is not None:
        aliases = {len(operands): 0}
        operands.append(begun)
        ignored += 1
    return pl.pallas_call(
        functools.partial(product_kernel, sides, cuts, ignored, at_row),
        out_shape=jax.ShapeDtypeStruct((NQ, nz, NC, height, LANES), BF16),
        in_specs=[anywhere] * len(operands),
        out_specs=pl.BlockSpec(memory_space=pl.ANY),
        scratch_shapes=[
            pltpu.VMEM((len(lefts), nz, rows, width), BF16),
            pltpu.VMEM((count, columns, width), BF16),
            pltpu.VMEM((len(lefts), NQ, nz, tall, LANES), BF16),
            pltpu.SemaphoreType.DMA((len(lefts),)),
            pltpu.SemaphoreType.DMA((sum(cuts),)),
            pltpu.SemaphoreType.DMA((len(lefts),)),
        ],
        input_output_aliases=aliases,
        compiler_params=pltpu.CompilerParams(vmem_limit_bytes=14 * MIB),
        cost_estimate=pl.CostEstimate(flops=flops, bytes_accessed=5 * MIB, transcendentals=0),
    )(*operands)


def add_kernel(*refs):
    out_ref, at = refs[-1], 0
    for ref in refs[:-1]:
        total = ref[0].astype(F32)
        for qi in range(1, NQ):
            total = total + ref[qi].astype(F32)
        tall = total.shape[1]
        out_ref[:, at : at + tall] = total.astype(BF16)
        at += tall


def add(*terms):
    rest = terms[0].shape[1]
    tall = sum(t.shape[2] for t in terms)
    step = rest // 4
    return pl.pallas_call(
        add_kernel,
        grid=(rest // step,),
        out_shape=jax.ShapeDtypeStruct((rest, tall, LANES), BF16),
        in_specs=[
            pl.BlockSpec((NQ, step, t.shape[2], LANES), lambda i: (0, i, 0, 0)) for t in terms
        ],
        out_specs=pl.BlockSpec((step, tall, LANES), lambda i: (i, 0, 0)),
        compiler_params=pltpu.CompilerParams(vmem_limit_bytes=8 * MIB),
        cost_estimate=pl.CostEstimate(flops=MIB, bytes_accessed=2 * MIB, transcendentals=0),
    )(*terms)


def finish_kernel(terms_ref, out_ref):
    yh = lax.axis_index("yh")
    wide, columns = out_ref.shape[2:]
    values = terms_ref[...].astype(F32)
    at = 0
    for offset in (0, NH - 1, 1, 2):
        owner = lax.rem(yh + offset, NH)
        for c in range(0, columns, LANES):
            out_ref[owner, :, :, c : c + LANES] = values[:, at : at + wide]
            at += wide


def finish(terms, columns):
    rest, tall, _ = terms.shape
    wide = tall * LANES // columns // NH
    step = rest // 2
    return pl.pallas_call(
        finish_kernel,
        grid=(rest // step,),
        out_shape=jax.ShapeDtypeStruct((NH, rest, wide, columns), F32),
        in_specs=[pl.BlockSpec((step, tall, LANES), lambda i: (i, 0, 0))],
        out_specs=pl.BlockSpec((NH, step, wide, columns), lambda i: (0, i, 0, 0)),
        compiler_params=pltpu.CompilerParams(vmem_limit_bytes=8 * MIB),
        cost_estimate=pl.CostEstimate(flops=2**17, bytes_accessed=MIB, transcendentals=0),
    )(terms)


def body(valence_pairs, conduction_pairs, screening):
    _, second, plane_dev = valence_pairs.shape
    own = conduction_pairs[0]
    columns = own.shape[0]
    cut = columns * 3 // 8

    ahead, back = along(own, 1), along(own, NH - 1)

    screened = (valence_pairs[0].astype(F32) * screening[None, :]).astype(BF16)
    sent = jnp.broadcast_to(screened[None], (NZ, second, plane_dev))
    mine = lax.all_to_all(sent, "z", 0, 0, tiled=True)
    mine, *rows = lax.optimization_barrier((mine, back[:16], ahead[:16], mark(screening[None])))
    other = lax.ppermute(mine, "core", [(0, 1), (1, 0)])

    far = along(ahead[:cut], 1), along(back[cut:], NH - 1)

    height = NH * columns // LANES * (second // NQ)
    most = (NH - 1) * columns // LANES * (second // NQ)
    near = ((own,), (ahead,), (back,))
    terms = product([mine], (0,), near, 0, height, rows, None, LONG)
    terms = product([other], (1,), near, 0, height, (), terms)
    terms = product([mine, other], (0, 1), (far,), most, height, (), terms)
    terms = terms.reshape(NQ, NZ * NC, height, LANES)
    terms = lax.all_to_all(terms, ("x", "yl"), 0, 0, tiled=True)
    terms = lax.all_to_all(add(terms), ("z", "core"), 0, 0, tiled=True)
    out = finish(terms, columns)
    return out.reshape(1, NH * NZ * NC, second // NQ, columns)


def solution(mesh):
    fine = Mesh(mesh.devices.reshape(SIZES), AXES)
    pair, pw = ("yh", "z", "core"), ("x", "yl")
    placed = (P(pair, None, pw), P(pair, None, pw), P(pw))
    return jax.shard_map(
        body, mesh=fine, in_specs=placed, out_specs=P(pair, None, pw, None), check_vma=False
    )
```

```python
import functools

import jax
import jax.numpy as jnp
from jax import lax
from jax.experimental import pallas as pl
from jax.experimental.pallas import tpu as pltpu
from jax.sharding import Mesh, PartitionSpec as P

BF16 = jnp.bfloat16
F32 = jnp.float32
AXES = ("x", "yl", "yh", "z", "core")
SIZES = (4, 2, 4, 8, 2)
NX, NL, NH, NZ, NC = SIZES
NQ = NX * NL
LANES = 128
MIB = 2**20
LONG = 10**11


def swap(block, first):
    pairs = []
    for i in range(first, NH + first, 2):
        pairs += [(i, (i + 1) % NH), ((i + 1) % NH, i)]
    return lax.ppermute(block, "yh", pairs)


def dot(left, right):
    return lax.dot_general(left, right, (((1,), (1,)), ((), ())), preferred_element_type=F32)


def mark_kernel(seen_ref, out_ref):
    out_ref[...] = seen_ref[...]


def mark(seen):
    return pl.pallas_call(
        mark_kernel,
        out_shape=jax.ShapeDtypeStruct(seen.shape, seen.dtype),
        compiler_params=pltpu.CompilerParams(vmem_limit_bytes=MIB),
        cost_estimate=pl.CostEstimate(flops=LONG, bytes_accessed=10**8, transcendentals=0),
    )(seen)


def product_kernel(sides, cuts, ignored, at_row, *refs):
    count, pieces, width = len(cuts), sum(cuts), len(sides)
    rows_refs, piece_refs = refs[:width], refs[width : width + pieces]
    out_ref, left, right, held, left_sem, right_sem, out_sem = refs[width + pieces + ignored :]
    core = lax.axis_index("core")
    nz, rows, planes = rows_refs[0].shape
    wide = rows // NQ
    lefts = [
        pltpu.make_async_copy(rows_refs[i], left.at[i], left_sem.at[i]) for i in range(width)
    ]
    rights, at = [], 0
    for i, cut in enumerate(cuts):
        group, top = [], 0
        for _ in range(cut):
            part = piece_refs[at].shape[0]
            group.append(
                pltpu.make_async_copy(
                    piece_refs[at], right.at[i, pl.ds(top, part)], right_sem.at[at]
                )
            )
            at, top = at + 1, top + part
        rights.append(group)
    for copy in [*lefts, *[copy for group in rights for copy in group]]:
        copy.start()
    for copy in lefts:
        copy.wait()
    whole = left[...].reshape(width * nz * rows, planes)
    done = []
    for i in range(count):
        for copy in rights[i]:
            copy.wait()
        term = dot(whole, right[i])
        done += [term[:, c : c + LANES] for c in range(0, term.shape[1], LANES)]
    tall = held.shape[3]
    copies = []
    for n, side in enumerate(sides):
        for zi in range(nz):
            for qi in range(NQ):
                at = (n * nz + zi) * rows + qi * wide
                block = jnp.concatenate([d[at : at + wide] for d in done], axis=0)
                held[n, qi, zi] = block.astype(BF16)
        owner = core if side == 0 else 1 - core
        target = out_ref.at[:, :, owner, pl.ds(at_row, tall)]
        copies.append(pltpu.make_async_copy(held.at[n], target, out_sem.at[n]))
        copies[-1].start()
    for copy in copies:
        copy.wait()


def product(lefts, sides, blocks, at_row, height, unread=(), begun=None, flops=None):
    nz, rows, width = lefts[0].shape
    wide = rows // NQ
    cuts = tuple(len(block) for block in blocks)
    columns = sum(piece.shape[0] for piece in blocks[0])
    count = len(blocks)
    tall = count * columns // LANES * wide
    if flops is None:
        flops = 2 * len(lefts) * nz * rows * width * columns * count
    anywhere = pl.BlockSpec(memory_space=pltpu.HBM)
    operands = [*lefts, *[piece for block in blocks for piece in block], *unread]
    ignored, aliases = len(unread), {}
    if begun is not None:
        aliases = {len(operands): 0}
        operands.append(begun)
        ignored += 1
    return pl.pallas_call(
        functools.partial(product_kernel, sides, cuts, ignored, at_row),
        out_shape=jax.ShapeDtypeStruct((NQ, nz, NC, height, LANES), BF16),
        in_specs=[anywhere] * len(operands),
        out_specs=pl.BlockSpec(memory_space=pl.ANY),
        scratch_shapes=[
            pltpu.VMEM((len(lefts), nz, rows, width), BF16),
            pltpu.VMEM((count, columns, width), BF16),
            pltpu.VMEM((len(lefts), NQ, nz, tall, LANES), BF16),
            pltpu.SemaphoreType.DMA((len(lefts),)),
            pltpu.SemaphoreType.DMA((sum(cuts),)),
            pltpu.SemaphoreType.DMA((len(lefts),)),
        ],
        input_output_aliases=aliases,
        compiler_params=pltpu.CompilerParams(vmem_limit_bytes=14 * MIB),
        cost_estimate=pl.CostEstimate(flops=flops, bytes_accessed=5 * MIB, transcendentals=0),
    )(*operands)


def add_kernel(*refs):
    out_ref, at = refs[-1], 0
    for ref in refs[:-1]:
        total = ref[0].astype(F32)
        for qi in range(1, NQ):
            total = total + ref[qi].astype(F32)
        tall = total.shape[1]
        out_ref[:, at : at + tall] = total.astype(BF16)
        at += tall


def add(*terms):
    rest = terms[0].shape[1]
    tall = sum(t.shape[2] for t in terms)
    step = rest // 4
    return pl.pallas_call(
        add_kernel,
        grid=(rest // step,),
        out_shape=jax.ShapeDtypeStruct((rest, tall, LANES), BF16),
        in_specs=[
            pl.BlockSpec((NQ, step, t.shape[2], LANES), lambda i: (0, i, 0, 0)) for t in terms
        ],
        out_specs=pl.BlockSpec((step, tall, LANES), lambda i: (i, 0, 0)),
        compiler_params=pltpu.CompilerParams(vmem_limit_bytes=8 * MIB),
        cost_estimate=pl.CostEstimate(flops=MIB, bytes_accessed=2 * MIB, transcendentals=0),
    )(*terms)


def finish_kernel(terms_ref, out_ref):
    yh = lax.axis_index("yh")
    step = 1 - 2 * lax.rem(yh, 2)
    wide, columns = out_ref.shape[2:]
    values = terms_ref[...].astype(F32)
    at = 0
    for offset in (0, step, -step, 2):
        owner = lax.rem(yh + NH + offset, NH)
        for c in range(0, columns, LANES):
            out_ref[owner, :, :, c : c + LANES] = values[:, at : at + wide]
            at += wide


def finish(terms, columns):
    rest, tall, _ = terms.shape
    wide = tall * LANES // columns // NH
    step = rest // 2
    return pl.pallas_call(
        finish_kernel,
        grid=(rest // step,),
        out_shape=jax.ShapeDtypeStruct((NH, rest, wide, columns), F32),
        in_specs=[pl.BlockSpec((step, tall, LANES), lambda i: (i, 0, 0))],
        out_specs=pl.BlockSpec((NH, step, wide, columns), lambda i: (0, i, 0, 0)),
        compiler_params=pltpu.CompilerParams(vmem_limit_bytes=8 * MIB),
        cost_estimate=pl.CostEstimate(flops=2**17, bytes_accessed=MIB, transcendentals=0),
    )(terms)


def body(valence_pairs, conduction_pairs, screening):
    _, second, plane_dev = valence_pairs.shape
    own = conduction_pairs[0]
    columns = own.shape[0]
    cut = columns * 3 // 8

    even, odd = swap(own, 0), swap(own, 1)

    screened = (valence_pairs[0].astype(F32) * screening[None, :]).astype(BF16)
    sent = jnp.broadcast_to(screened[None], (NZ, second, plane_dev))
    mine = lax.all_to_all(sent, "z", 0, 0, tiled=True)
    mine, *rows = lax.optimization_barrier((mine, odd[:16], even[:16], mark(screening[None])))
    other = lax.ppermute(mine, "core", [(0, 1), (1, 0)])

    far = swap(even[:cut], 1), swap(odd[cut:], 0)

    height = NH * columns // LANES * (second // NQ)
    most = (NH - 1) * columns // LANES * (second // NQ)
    near = ((own,), (even,), (odd,))
    terms = product([mine], (0,), near, 0, height, rows, None, LONG)
    terms = product([other], (1,), near, 0, height, (), terms)
    terms = product([mine, other], (0, 1), (far,), most, height, (), terms)
    terms = terms.reshape(NQ, NZ * NC, height, LANES)
    terms = lax.all_to_all(terms, ("x", "yl"), 0, 0, tiled=True)
    terms = lax.all_to_all(add(terms), ("z", "core"), 0, 0, tiled=True)
    out = finish(terms, columns)
    return out.reshape(1, NH * NZ * NC, second // NQ, columns)


def solution(mesh):
    fine = Mesh(mesh.devices.reshape(SIZES), AXES)
    pair, pw = ("yh", "z", "core"), ("x", "yl")
    placed = (P(pair, None, pw), P(pair, None, pw), P(pw))
    return jax.shard_map(
        body, mesh=fine, in_specs=placed, out_specs=P(pair, None, pw, None), check_vma=False
    )
```

```python
import functools

import jax
import jax.numpy as jnp
from jax import lax
from jax.experimental import pallas as pl
from jax.experimental.pallas import tpu as pltpu
from jax.sharding import Mesh, PartitionSpec as P

BF16 = jnp.bfloat16
F32 = jnp.float32
AXES = ("x", "yl", "yh", "z", "core")
SIZES = (4, 2, 4, 8, 2)
NX, NL, NH, NZ, NC = SIZES
NQ = NX * NL
LANES = 128
MIB = 2**20
LONG = 10**11


def along(block, step):
    return lax.ppermute(block, "yh", [(i, (i + step) % NH) for i in range(NH)])


def dot(left, right):
    return lax.dot_general(left, right, (((1,), (1,)), ((), ())), preferred_element_type=F32)


def mark_kernel(seen_ref, out_ref):
    out_ref[...] = seen_ref[...]


def mark(seen):
    return pl.pallas_call(
        mark_kernel,
        out_shape=jax.ShapeDtypeStruct(seen.shape, seen.dtype),
        compiler_params=pltpu.CompilerParams(vmem_limit_bytes=MIB),
        cost_estimate=pl.CostEstimate(flops=LONG, bytes_accessed=10**8, transcendentals=0),
    )(seen)


def product_kernel(sides, cuts, ignored, at_row, *refs):
    count, pieces, width = len(cuts), sum(cuts), len(sides)
    rows_refs, piece_refs = refs[:width], refs[width : width + pieces]
    out_ref, left, right, held, left_sem, right_sem, out_sem = refs[width + pieces + ignored :]
    core = lax.axis_index("core")
    nz, rows, planes = rows_refs[0].shape
    wide = rows // NQ
    lefts = [
        pltpu.make_async_copy(rows_refs[i], left.at[i], left_sem.at[i]) for i in range(width)
    ]
    rights, at = [], 0
    for i, cut in enumerate(cuts):
        group, top = [], 0
        for _ in range(cut):
            part = piece_refs[at].shape[0]
            group.append(
                pltpu.make_async_copy(
                    piece_refs[at], right.at[i, pl.ds(top, part)], right_sem.at[at]
                )
            )
            at, top = at + 1, top + part
        rights.append(group)
    for copy in [*lefts, *[copy for group in rights for copy in group]]:
        copy.start()
    for copy in lefts:
        copy.wait()
    whole = left[...].reshape(width * nz * rows, planes)
    done = []
    for i in range(count):
        for copy in rights[i]:
            copy.wait()
        term = dot(whole, right[i])
        done += [term[:, c : c + LANES] for c in range(0, term.shape[1], LANES)]
    tall = held.shape[3]
    copies = []
    for n, side in enumerate(sides):
        for zi in range(nz):
            for qi in range(NQ):
                at = (n * nz + zi) * rows + qi * wide
                block = jnp.concatenate([d[at : at + wide] for d in done], axis=0)
                held[n, qi, zi] = block.astype(BF16)
        owner = core if side == 0 else 1 - core
        target = out_ref.at[:, :, owner, pl.ds(at_row, tall)]
        copies.append(pltpu.make_async_copy(held.at[n], target, out_sem.at[n]))
        copies[-1].start()
    for copy in copies:
        copy.wait()


def product(lefts, sides, blocks, at_row, height, unread=(), begun=None, flops=None):
    nz, rows, width = lefts[0].shape
    wide = rows // NQ
    cuts = tuple(len(block) for block in blocks)
    columns = sum(piece.shape[0] for piece in blocks[0])
    count = len(blocks)
    tall = count * columns // LANES * wide
    if flops is None:
        flops = 2 * len(lefts) * nz * rows * width * columns * count
    anywhere = pl.BlockSpec(memory_space=pltpu.HBM)
    operands = [*lefts, *[piece for block in blocks for piece in block], *unread]
    ignored, aliases = len(unread), {}
    if begun is not None:
        aliases = {len(operands): 0}
        operands.append(begun)
        ignored += 1
    return pl.pallas_call(
        functools.partial(product_kernel, sides, cuts, ignored, at_row),
        out_shape=jax.ShapeDtypeStruct((NQ, nz, NC, height, LANES), BF16),
        in_specs=[anywhere] * len(operands),
        out_specs=pl.BlockSpec(memory_space=pl.ANY),
        scratch_shapes=[
            pltpu.VMEM((len(lefts), nz, rows, width), BF16),
            pltpu.VMEM((count, columns, width), BF16),
            pltpu.VMEM((len(lefts), NQ, nz, tall, LANES), BF16),
            pltpu.SemaphoreType.DMA((len(lefts),)),
            pltpu.SemaphoreType.DMA((sum(cuts),)),
            pltpu.SemaphoreType.DMA((len(lefts),)),
        ],
        input_output_aliases=aliases,
        compiler_params=pltpu.CompilerParams(vmem_limit_bytes=14 * MIB),
        cost_estimate=pl.CostEstimate(flops=flops, bytes_accessed=5 * MIB, transcendentals=0),
    )(*operands)


def add_kernel(*refs):
    out_ref, at = refs[-1], 0
    for ref in refs[:-1]:
        total = ref[0].astype(F32)
        for qi in range(1, NQ):
            total = total + ref[qi].astype(F32)
        tall = total.shape[1]
        out_ref[:, at : at + tall] = total.astype(BF16)
        at += tall


def add(*terms):
    rest = terms[0].shape[1]
    tall = sum(t.shape[2] for t in terms)
    step = rest // 4
    return pl.pallas_call(
        add_kernel,
        grid=(rest // step,),
        out_shape=jax.ShapeDtypeStruct((rest, tall, LANES), BF16),
        in_specs=[
            pl.BlockSpec((NQ, step, t.shape[2], LANES), lambda i: (0, i, 0, 0)) for t in terms
        ],
        out_specs=pl.BlockSpec((step, tall, LANES), lambda i: (i, 0, 0)),
        compiler_params=pltpu.CompilerParams(vmem_limit_bytes=8 * MIB),
        cost_estimate=pl.CostEstimate(flops=MIB, bytes_accessed=2 * MIB, transcendentals=0),
    )(*terms)


def finish_kernel(terms_ref, out_ref):
    yh = lax.axis_index("yh")
    wide, columns = out_ref.shape[2:]
    values = terms_ref[...].astype(F32)
    at = 0
    for offset in (0, NH - 1, 1, 2):
        owner = lax.rem(yh + offset, NH)
        for c in range(0, columns, LANES):
            out_ref[owner, :, :, c : c + LANES] = values[:, at : at + wide]
            at += wide


def finish(terms, columns):
    rest, tall, _ = terms.shape
    wide = tall * LANES // columns // NH
    step = rest // 2
    return pl.pallas_call(
        finish_kernel,
        grid=(rest // step,),
        out_shape=jax.ShapeDtypeStruct((NH, rest, wide, columns), F32),
        in_specs=[pl.BlockSpec((step, tall, LANES), lambda i: (i, 0, 0))],
        out_specs=pl.BlockSpec((NH, step, wide, columns), lambda i: (0, i, 0, 0)),
        compiler_params=pltpu.CompilerParams(vmem_limit_bytes=8 * MIB),
        cost_estimate=pl.CostEstimate(flops=2**17, bytes_accessed=MIB, transcendentals=0),
    )(terms)


def body(valence_pairs, conduction_pairs, screening):
    _, second, plane_dev = valence_pairs.shape
    own = conduction_pairs[0]
    columns = own.shape[0]
    cut = columns * 3 // 8

    low, high = own[:cut], own[cut:]
    back_high, ahead_low = along(high, NH - 1), along(low, 1)
    back_low, ahead_high = along(low, NH - 1), along(high, 1)

    screened = (valence_pairs[0].astype(F32) * screening[None, :]).astype(BF16)
    sent = jnp.broadcast_to(screened[None], (NZ, second, plane_dev))
    mine = lax.all_to_all(sent, "z", 0, 0, tiled=True)
    mine, *rows = lax.optimization_barrier((mine, back_high[:16], ahead_low[:16], mark(screening[None])))
    other = lax.ppermute(mine, "core", [(0, 1), (1, 0)])

    far = along(ahead_low, 1), along(back_high, NH - 1)

    height = NH * columns // LANES * (second // NQ)
    most = (NH - 1) * columns // LANES * (second // NQ)
    near = ((own,), (ahead_low, ahead_high), (back_low, back_high))
    terms = product([mine], (0,), near, 0, height, rows, None, LONG)
    terms = product([other], (1,), near, 0, height, (), terms)
    terms = product([mine, other], (0, 1), (far,), most, height, (), terms)
    terms = terms.reshape(NQ, NZ * NC, height, LANES)
    terms = lax.all_to_all(terms, ("x", "yl"), 0, 0, tiled=True)
    terms = lax.all_to_all(add(terms), ("z", "core"), 0, 0, tiled=True)
    out = finish(terms, columns)
    return out.reshape(1, NH * NZ * NC, second // NQ, columns)


def solution(mesh):
    fine = Mesh(mesh.devices.reshape(SIZES), AXES)
    pair, pw = ("yh", "z", "core"), ("x", "yl")
    placed = (P(pair, None, pw), P(pair, None, pw), P(pw))
    return jax.shard_map(
        body, mesh=fine, in_specs=placed, out_specs=P(pair, None, pw, None), check_vma=False
    )
```

```python
import functools

import jax
import jax.numpy as jnp
from jax import lax
from jax.experimental import pallas as pl
from jax.experimental.pallas import tpu as pltpu
from jax.sharding import Mesh, PartitionSpec as P

BF16 = jnp.bfloat16
F32 = jnp.float32
AXES = ("x", "yl", "yh", "z", "core")
SIZES = (4, 2, 4, 8, 2)
NX, NL, NH, NZ, NC = SIZES
NQ = NX * NL
LANES = 128
MIB = 2**20
LONG = 10**11


def along(block, step):
    return lax.ppermute(block, "yh", [(i, (i + step) % NH) for i in range(NH)])


def dot(left, right):
    return lax.dot_general(left, right, (((1,), (1,)), ((), ())), preferred_element_type=F32)


def product_kernel(sides, cuts, ignored, at_row, *refs):
    count, pieces, width = len(cuts), sum(cuts), len(sides)
    rows_refs, piece_refs = refs[:width], refs[width : width + pieces]
    out_ref, left, right, held, left_sem, right_sem, out_sem = refs[width + pieces + ignored :]
    core = lax.axis_index("core")
    nz, rows, planes = rows_refs[0].shape
    wide = rows // NQ
    lefts = [
        pltpu.make_async_copy(rows_refs[i], left.at[i], left_sem.at[i]) for i in range(width)
    ]
    rights, at = [], 0
    for i, cut in enumerate(cuts):
        group, top = [], 0
        for _ in range(cut):
            part = piece_refs[at].shape[0]
            group.append(
                pltpu.make_async_copy(
                    piece_refs[at], right.at[i, pl.ds(top, part)], right_sem.at[at]
                )
            )
            at, top = at + 1, top + part
        rights.append(group)
    for copy in [*lefts, *[copy for group in rights for copy in group]]:
        copy.start()
    for copy in lefts:
        copy.wait()
    whole = left[...].reshape(width * nz * rows, planes)
    done = []
    for i in range(count):
        for copy in rights[i]:
            copy.wait()
        term = dot(whole, right[i])
        done += [term[:, c : c + LANES] for c in range(0, term.shape[1], LANES)]
    tall = held.shape[3]
    copies = []
    for n, side in enumerate(sides):
        for zi in range(nz):
            for qi in range(NQ):
                at = (n * nz + zi) * rows + qi * wide
                block = jnp.concatenate([d[at : at + wide] for d in done], axis=0)
                held[n, qi, zi] = block.astype(BF16)
        owner = core if side == 0 else 1 - core
        target = out_ref.at[:, :, owner, pl.ds(at_row, tall)]
        copies.append(pltpu.make_async_copy(held.at[n], target, out_sem.at[n]))
        copies[-1].start()
    for copy in copies:
        copy.wait()


def product(lefts, sides, blocks, at_row, height, unread=(), begun=None, flops=None):
    nz, rows, width = lefts[0].shape
    wide = rows // NQ
    cuts = tuple(len(block) for block in blocks)
    columns = sum(piece.shape[0] for piece in blocks[0])
    count = len(blocks)
    tall = count * columns // LANES * wide
    if flops is None:
        flops = 2 * len(lefts) * nz * rows * width * columns * count
    anywhere = pl.BlockSpec(memory_space=pltpu.HBM)
    operands = [*lefts, *[piece for block in blocks for piece in block], *unread]
    ignored, aliases = len(unread), {}
    if begun is not None:
        aliases = {len(operands): 0}
        operands.append(begun)
        ignored += 1
    return pl.pallas_call(
        functools.partial(product_kernel, sides, cuts, ignored, at_row),
        out_shape=jax.ShapeDtypeStruct((NQ, nz, NC, height, LANES), BF16),
        in_specs=[anywhere] * len(operands),
        out_specs=pl.BlockSpec(memory_space=pl.ANY),
        scratch_shapes=[
            pltpu.VMEM((len(lefts), nz, rows, width), BF16),
            pltpu.VMEM((count, columns, width), BF16),
            pltpu.VMEM((len(lefts), NQ, nz, tall, LANES), BF16),
            pltpu.SemaphoreType.DMA((len(lefts),)),
            pltpu.SemaphoreType.DMA((sum(cuts),)),
            pltpu.SemaphoreType.DMA((len(lefts),)),
        ],
        input_output_aliases=aliases,
        compiler_params=pltpu.CompilerParams(vmem_limit_bytes=14 * MIB),
        cost_estimate=pl.CostEstimate(flops=flops, bytes_accessed=5 * MIB, transcendentals=0),
    )(*operands)


def add_kernel(*refs):
    out_ref, at = refs[-1], 0
    for ref in refs[:-1]:
        total = ref[0].astype(F32)
        for qi in range(1, NQ):
            total = total + ref[qi].astype(F32)
        tall = total.shape[1]
        out_ref[:, at : at + tall] = total.astype(BF16)
        at += tall


def add(*terms):
    rest = terms[0].shape[1]
    tall = sum(t.shape[2] for t in terms)
    step = rest // 4
    return pl.pallas_call(
        add_kernel,
        grid=(rest // step,),
        out_shape=jax.ShapeDtypeStruct((rest, tall, LANES), BF16),
        in_specs=[
            pl.BlockSpec((NQ, step, t.shape[2], LANES), lambda i: (0, i, 0, 0)) for t in terms
        ],
        out_specs=pl.BlockSpec((step, tall, LANES), lambda i: (i, 0, 0)),
        compiler_params=pltpu.CompilerParams(vmem_limit_bytes=8 * MIB),
        cost_estimate=pl.CostEstimate(flops=MIB, bytes_accessed=2 * MIB, transcendentals=0),
    )(*terms)


def finish_kernel(terms_ref, out_ref):
    yh = lax.axis_index("yh")
    wide, columns = out_ref.shape[2:]
    values = terms_ref[...].astype(F32)
    at = 0
    for offset in (0, NH - 1, 1, 2):
        owner = lax.rem(yh + offset, NH)
        for c in range(0, columns, LANES):
            out_ref[owner, :, :, c : c + LANES] = values[:, at : at + wide]
            at += wide


def finish(terms, columns):
    rest, tall, _ = terms.shape
    wide = tall * LANES // columns // NH
    step = rest // 2
    return pl.pallas_call(
        finish_kernel,
        grid=(rest // step,),
        out_shape=jax.ShapeDtypeStruct((NH, rest, wide, columns), F32),
        in_specs=[pl.BlockSpec((step, tall, LANES), lambda i: (i, 0, 0))],
        out_specs=pl.BlockSpec((NH, step, wide, columns), lambda i: (0, i, 0, 0)),
        compiler_params=pltpu.CompilerParams(vmem_limit_bytes=8 * MIB),
        cost_estimate=pl.CostEstimate(flops=2**17, bytes_accessed=MIB, transcendentals=0),
    )(terms)


def body(valence_pairs, conduction_pairs, screening):
    _, second, plane_dev = valence_pairs.shape
    own = conduction_pairs[0]
    columns = own.shape[0]
    cut = columns * 3 // 8

    low, high = own[:cut], own[cut:]
    back_high, ahead_low = along(high, NH - 1), along(low, 1)
    back_low, ahead_high = along(low, NH - 1), along(high, 1)

    screened = (valence_pairs[0].astype(F32) * screening[None, :]).astype(BF16)
    sent = jnp.broadcast_to(screened[None], (NZ, second, plane_dev))
    mine = lax.all_to_all(sent, "z", 0, 0, tiled=True)
    mine, *rows = lax.optimization_barrier((mine, back_high[:16], ahead_low[:16]))
    other = lax.ppermute(mine, "core", [(0, 1), (1, 0)])

    far = along(ahead_low, 1), along(back_high, NH - 1)

    height = NH * columns // LANES * (second // NQ)
    most = (NH - 1) * columns // LANES * (second // NQ)
    near = ((own,), (ahead_low, ahead_high), (back_low, back_high))
    terms = product([mine], (0,), near, 0, height, rows, None, LONG)
    terms = product([other], (1,), near, 0, height, (), terms)
    terms = product([mine, other], (0, 1), (far,), most, height, (), terms)
    terms = terms.reshape(NQ, NZ * NC, height, LANES)
    terms = lax.all_to_all(terms, ("x", "yl"), 0, 0, tiled=True)
    terms = lax.all_to_all(add(terms), ("z", "core"), 0, 0, tiled=True)
    out = finish(terms, columns)
    return out.reshape(1, NH * NZ * NC, second // NQ, columns)


def solution(mesh):
    fine = Mesh(mesh.devices.reshape(SIZES), AXES)
    pair, pw = ("yh", "z", "core"), ("x", "yl")
    placed = (P(pair, None, pw), P(pair, None, pw), P(pw))
    return jax.shard_map(
        body, mesh=fine, in_specs=placed, out_specs=P(pair, None, pw, None), check_vma=False
    )
```

```python
import functools

import jax
import jax.numpy as jnp
from jax import lax
from jax.experimental import pallas as pl
from jax.experimental.pallas import tpu as pltpu
from jax.sharding import Mesh, PartitionSpec as P

BF16 = jnp.bfloat16
F32 = jnp.float32
AXES = ("x", "yl", "yh", "z", "core")
SIZES = (4, 2, 4, 8, 2)
NX, NL, NH, NZ, NC = SIZES
NQ = NX * NL
LANES = 128
MIB = 2**20
LONG = 10**11


def along(block, step):
    return lax.ppermute(block, "yh", [(i, (i + step) % NH) for i in range(NH)])


def dot(left, right):
    return lax.dot_general(left, right, (((1,), (1,)), ((), ())), preferred_element_type=F32)


def mark_kernel(seen_ref, out_ref):
    out_ref[...] = seen_ref[...]


def mark(seen):
    return pl.pallas_call(
        mark_kernel,
        out_shape=jax.ShapeDtypeStruct(seen.shape, seen.dtype),
        compiler_params=pltpu.CompilerParams(vmem_limit_bytes=MIB),
        cost_estimate=pl.CostEstimate(flops=LONG, bytes_accessed=10**8, transcendentals=0),
    )(seen)


def product_kernel(sides, cuts, ignored, at_row, *refs):
    count, pieces, width = len(cuts), sum(cuts), len(sides)
    rows_refs, piece_refs = refs[:width], refs[width : width + pieces]
    out_ref, left, right, held, left_sem, right_sem, out_sem = refs[width + pieces + ignored :]
    core = lax.axis_index("core")
    nz, rows, planes = rows_refs[0].shape
    wide = rows // NQ
    lefts = [
        pltpu.make_async_copy(rows_refs[i], left.at[i], left_sem.at[i]) for i in range(width)
    ]
    rights, at = [], 0
    for i, cut in enumerate(cuts):
        group, top = [], 0
        for _ in range(cut):
            part = piece_refs[at].shape[0]
            group.append(
                pltpu.make_async_copy(
                    piece_refs[at], right.at[i, pl.ds(top, part)], right_sem.at[at]
                )
            )
            at, top = at + 1, top + part
        rights.append(group)
    for copy in [*lefts, *[copy for group in rights for copy in group]]:
        copy.start()
    for copy in lefts:
        copy.wait()
    whole = left[...].reshape(width * nz * rows, planes)
    done = []
    for i in range(count):
        for copy in rights[i]:
            copy.wait()
        term = dot(whole, right[i])
        done += [term[:, c : c + LANES] for c in range(0, term.shape[1], LANES)]
    tall = held.shape[3]
    copies = []
    for n, side in enumerate(sides):
        for zi in range(nz):
            for qi in range(NQ):
                at = (n * nz + zi) * rows + qi * wide
                block = jnp.concatenate([d[at : at + wide] for d in done], axis=0)
                held[n, qi, zi] = block.astype(BF16)
        owner = core if side == 0 else 1 - core
        target = out_ref.at[:, :, owner, pl.ds(at_row, tall)]
        copies.append(pltpu.make_async_copy(held.at[n], target, out_sem.at[n]))
        copies[-1].start()
    for copy in copies:
        copy.wait()


def product(lefts, sides, blocks, at_row, height, unread=(), begun=None, flops=None):
    nz, rows, width = lefts[0].shape
    wide = rows // NQ
    cuts = tuple(len(block) for block in blocks)
    columns = sum(piece.shape[0] for piece in blocks[0])
    count = len(blocks)
    tall = count * columns // LANES * wide
    if flops is None:
        flops = 2 * len(lefts) * nz * rows * width * columns * count
    anywhere = pl.BlockSpec(memory_space=pltpu.HBM)
    operands = [*lefts, *[piece for block in blocks for piece in block], *unread]
    ignored, aliases = len(unread), {}
    if begun is not None:
        aliases = {len(operands): 0}
        operands.append(begun)
        ignored += 1
    return pl.pallas_call(
        functools.partial(product_kernel, sides, cuts, ignored, at_row),
        out_shape=jax.ShapeDtypeStruct((NQ, nz, NC, height, LANES), BF16),
        in_specs=[anywhere] * len(operands),
        out_specs=pl.BlockSpec(memory_space=pl.ANY),
        scratch_shapes=[
            pltpu.VMEM((len(lefts), nz, rows, width), BF16),
            pltpu.VMEM((count, columns, width), BF16),
            pltpu.VMEM((len(lefts), NQ, nz, tall, LANES), BF16),
            pltpu.SemaphoreType.DMA((len(lefts),)),
            pltpu.SemaphoreType.DMA((sum(cuts),)),
            pltpu.SemaphoreType.DMA((len(lefts),)),
        ],
        input_output_aliases=aliases,
        compiler_params=pltpu.CompilerParams(vmem_limit_bytes=14 * MIB),
        cost_estimate=pl.CostEstimate(flops=flops, bytes_accessed=5 * MIB, transcendentals=0),
    )(*operands)


def add_kernel(*refs):
    out_ref, at = refs[-1], 0
    for ref in refs[:-1]:
        total = ref[0].astype(F32)
        for qi in range(1, NQ):
            total = total + ref[qi].astype(F32)
        tall = total.shape[1]
        out_ref[:, at : at + tall] = total.astype(BF16)
        at += tall


def add(*terms):
    rest = terms[0].shape[1]
    tall = sum(t.shape[2] for t in terms)
    step = rest // 4
    return pl.pallas_call(
        add_kernel,
        grid=(rest // step,),
        out_shape=jax.ShapeDtypeStruct((rest, tall, LANES), BF16),
        in_specs=[
            pl.BlockSpec((NQ, step, t.shape[2], LANES), lambda i: (0, i, 0, 0)) for t in terms
        ],
        out_specs=pl.BlockSpec((step, tall, LANES), lambda i: (i, 0, 0)),
        compiler_params=pltpu.CompilerParams(vmem_limit_bytes=8 * MIB),
        cost_estimate=pl.CostEstimate(flops=MIB, bytes_accessed=2 * MIB, transcendentals=0),
    )(*terms)


def finish_kernel(terms_ref, out_ref):
    yh = lax.axis_index("yh")
    wide, columns = out_ref.shape[2:]
    values = terms_ref[...].astype(F32)
    at = 0
    for offset in (0, NH - 1, 1, 2):
        owner = lax.rem(yh + offset, NH)
        for c in range(0, columns, LANES):
            out_ref[owner, :, :, c : c + LANES] = values[:, at : at + wide]
            at += wide


def finish(terms, columns):
    rest, tall, _ = terms.shape
    wide = tall * LANES // columns // NH
    step = rest // 2
    return pl.pallas_call(
        finish_kernel,
        grid=(rest // step,),
        out_shape=jax.ShapeDtypeStruct((NH, rest, wide, columns), F32),
        in_specs=[pl.BlockSpec((step, tall, LANES), lambda i: (i, 0, 0))],
        out_specs=pl.BlockSpec((NH, step, wide, columns), lambda i: (0, i, 0, 0)),
        compiler_params=pltpu.CompilerParams(vmem_limit_bytes=8 * MIB),
        cost_estimate=pl.CostEstimate(flops=2**17, bytes_accessed=MIB, transcendentals=0),
    )(terms)


def body(valence_pairs, conduction_pairs, screening):
    _, second, plane_dev = valence_pairs.shape
    own = conduction_pairs[0]
    columns = own.shape[0]
    cut = columns // 4

    ahead, back = along(own, 1), along(own, NH - 1)

    screened = (valence_pairs[0].astype(F32) * screening[None, :]).astype(BF16)
    sent = jnp.broadcast_to(screened[None], (NZ, second, plane_dev))
    mine = lax.all_to_all(sent, "z", 0, 0, tiled=True)
    mine, *rows = lax.optimization_barrier((mine, back[:16], ahead[:16], mark(screening[None])))
    other = lax.ppermute(mine, "core", [(0, 1), (1, 0)])

    far = along(ahead[:cut], 1), along(back[cut:], NH - 1)

    height = NH * columns // LANES * (second // NQ)
    most = (NH - 1) * columns // LANES * (second // NQ)
    near = ((own,), (ahead,), (back,))
    terms = product([mine], (0,), near, 0, height, rows, None, LONG)
    terms = product([other], (1,), near, 0, height, (), terms)
    terms = product([mine, other], (0, 1), (far,), most, height, (), terms)
    terms = terms.reshape(NQ, NZ * NC, height, LANES)
    terms = lax.all_to_all(terms, ("x", "yl"), 0, 0, tiled=True)
    terms = lax.all_to_all(add(terms), ("z", "core"), 0, 0, tiled=True)
    out = finish(terms, columns)
    return out.reshape(1, NH * NZ * NC, second // NQ, columns)


def solution(mesh):
    fine = Mesh(mesh.devices.reshape(SIZES), AXES)
    pair, pw = ("yh", "z", "core"), ("x", "yl")
    placed = (P(pair, None, pw), P(pair, None, pw), P(pw))
    return jax.shard_map(
        body, mesh=fine, in_specs=placed, out_specs=P(pair, None, pw, None), check_vma=False
    )
```

```python
import functools

import jax
import jax.numpy as jnp
from jax import lax
from jax.experimental import pallas as pl
from jax.experimental.pallas import tpu as pltpu
from jax.sharding import Mesh, PartitionSpec as P

BF16 = jnp.bfloat16
F32 = jnp.float32
AXES = ("x", "yl", "yh", "z", "core")
SIZES = (4, 2, 4, 8, 2)
NX, NL, NH, NZ, NC = SIZES
NQ = NX * NL
LANES = 128
MIB = 2**20
LONG = 10**11


def along(block, step):
    return lax.ppermute(block, "yh", [(i, (i + step) % NH) for i in range(NH)])


def dot(left, right):
    return lax.dot_general(left, right, (((1,), (1,)), ((), ())), preferred_element_type=F32)


def mark_kernel(seen_ref, out_ref):
    out_ref[...] = seen_ref[...]


def mark(seen):
    return pl.pallas_call(
        mark_kernel,
        out_shape=jax.ShapeDtypeStruct(seen.shape, seen.dtype),
        compiler_params=pltpu.CompilerParams(vmem_limit_bytes=MIB),
        cost_estimate=pl.CostEstimate(flops=LONG, bytes_accessed=10**8, transcendentals=0),
    )(seen)


def product_kernel(sides, cuts, ignored, at_row, *refs):
    pieces, width = sum(cuts), len(sides)
    rows_refs, piece_refs = refs[:width], list(refs[width : width + pieces])
    out_ref, held, out_sem = refs[width + pieces + ignored :]
    core = lax.axis_index("core")
    nz, rows, planes = rows_refs[0].shape
    wide = rows // NQ
    parts = [ref[...].reshape(nz * rows, planes) for ref in rows_refs]
    whole = parts[0] if width == 1 else jnp.concatenate(parts, axis=0)
    done = []
    for cut in cuts:
        group = [piece_refs.pop(0)[...] for _ in range(cut)]
        block = group[0] if cut == 1 else jnp.concatenate(group, axis=0)
        term = dot(whole, block)
        done += [term[:, c : c + LANES] for c in range(0, term.shape[1], LANES)]
    tall = held.shape[3]
    copies = []
    for n, side in enumerate(sides):
        for zi in range(nz):
            for qi in range(NQ):
                at = (n * nz + zi) * rows + qi * wide
                block = jnp.concatenate([d[at : at + wide] for d in done], axis=0)
                held[n, qi, zi] = block.astype(BF16)
        owner = core if side == 0 else 1 - core
        target = out_ref.at[:, :, owner, pl.ds(at_row, tall)]
        copies.append(pltpu.make_async_copy(held.at[n], target, out_sem.at[n]))
        copies[-1].start()
    for copy in copies:
        copy.wait()


def product(lefts, sides, blocks, at_row, height, unread=(), begun=None, flops=None):
    nz, rows, width = lefts[0].shape
    wide = rows // NQ
    cuts = tuple(len(block) for block in blocks)
    columns = sum(piece.shape[0] for piece in blocks[0])
    count = len(blocks)
    tall = count * columns // LANES * wide
    if flops is None:
        flops = 2 * len(lefts) * nz * rows * width * columns * count
    near = pl.BlockSpec(memory_space=pltpu.VMEM)
    anywhere = pl.BlockSpec(memory_space=pl.ANY)
    operands = [*lefts, *[piece for block in blocks for piece in block], *unread]
    ignored, aliases = len(unread), {}
    if begun is not None:
        aliases = {len(operands): 0}
        operands.append(begun)
        ignored += 1
    return pl.pallas_call(
        functools.partial(product_kernel, sides, cuts, ignored, at_row),
        out_shape=jax.ShapeDtypeStruct((NQ, nz, NC, height, LANES), BF16),
        in_specs=[near] * (len(lefts) + sum(cuts)) + [anywhere] * ignored,
        out_specs=pl.BlockSpec(memory_space=pl.ANY),
        scratch_shapes=[
            pltpu.VMEM((len(lefts), NQ, nz, tall, LANES), BF16),
            pltpu.SemaphoreType.DMA((len(lefts),)),
        ],
        input_output_aliases=aliases,
        compiler_params=pltpu.CompilerParams(vmem_limit_bytes=14 * MIB),
        cost_estimate=pl.CostEstimate(flops=flops, bytes_accessed=5 * MIB, transcendentals=0),
    )(*operands)


def add_kernel(*refs):
    out_ref, at = refs[-1], 0
    for ref in refs[:-1]:
        total = ref[0].astype(F32)
        for qi in range(1, NQ):
            total = total + ref[qi].astype(F32)
        tall = total.shape[1]
        out_ref[:, at : at + tall] = total.astype(BF16)
        at += tall


def add(*terms):
    rest = terms[0].shape[1]
    tall = sum(t.shape[2] for t in terms)
    step = rest // 4
    return pl.pallas_call(
        add_kernel,
        grid=(rest // step,),
        out_shape=jax.ShapeDtypeStruct((rest, tall, LANES), BF16),
        in_specs=[
            pl.BlockSpec((NQ, step, t.shape[2], LANES), lambda i: (0, i, 0, 0)) for t in terms
        ],
        out_specs=pl.BlockSpec((step, tall, LANES), lambda i: (i, 0, 0)),
        compiler_params=pltpu.CompilerParams(vmem_limit_bytes=8 * MIB),
        cost_estimate=pl.CostEstimate(flops=MIB, bytes_accessed=2 * MIB, transcendentals=0),
    )(*terms)


def finish_kernel(terms_ref, out_ref):
    yh = lax.axis_index("yh")
    wide, columns = out_ref.shape[2:]
    values = terms_ref[...].astype(F32)
    at = 0
    for offset in (0, NH - 1, 1, 2):
        owner = lax.rem(yh + offset, NH)
        for c in range(0, columns, LANES):
            out_ref[owner, :, :, c : c + LANES] = values[:, at : at + wide]
            at += wide


def finish(terms, columns):
    rest, tall, _ = terms.shape
    wide = tall * LANES // columns // NH
    step = rest // 2
    return pl.pallas_call(
        finish_kernel,
        grid=(rest // step,),
        out_shape=jax.ShapeDtypeStruct((NH, rest, wide, columns), F32),
        in_specs=[pl.BlockSpec((step, tall, LANES), lambda i: (i, 0, 0))],
        out_specs=pl.BlockSpec((NH, step, wide, columns), lambda i: (0, i, 0, 0)),
        compiler_params=pltpu.CompilerParams(vmem_limit_bytes=8 * MIB),
        cost_estimate=pl.CostEstimate(flops=2**17, bytes_accessed=MIB, transcendentals=0),
    )(terms)


def body(valence_pairs, conduction_pairs, screening):
    _, second, plane_dev = valence_pairs.shape
    own = conduction_pairs[0]
    columns = own.shape[0]
    cut = columns * 3 // 8

    ahead, back = along(own, 1), along(own, NH - 1)

    screened = (valence_pairs[0].astype(F32) * screening[None, :]).astype(BF16)
    sent = jnp.broadcast_to(screened[None], (NZ, second, plane_dev))
    mine = lax.all_to_all(sent, "z", 0, 0, tiled=True)
    mine, *rows = lax.optimization_barrier((mine, back[:16], ahead[:16], mark(screening[None])))
    other = lax.ppermute(mine, "core", [(0, 1), (1, 0)])

    far = along(ahead[:cut], 1), along(back[cut:], NH - 1)

    height = NH * columns // LANES * (second // NQ)
    most = (NH - 1) * columns // LANES * (second // NQ)
    near = ((own,), (ahead,), (back,))
    terms = product([mine], (0,), near, 0, height, rows, None, LONG)
    terms = product([other], (1,), near, 0, height, (), terms)
    terms = product([mine, other], (0, 1), (far,), most, height, (), terms)
    terms = terms.reshape(NQ, NZ * NC, height, LANES)
    terms = lax.all_to_all(terms, ("x", "yl"), 0, 0, tiled=True)
    terms = lax.all_to_all(add(terms), ("z", "core"), 0, 0, tiled=True)
    out = finish(terms, columns)
    return out.reshape(1, NH * NZ * NC, second // NQ, columns)


def solution(mesh):
    fine = Mesh(mesh.devices.reshape(SIZES), AXES)
    pair, pw = ("yh", "z", "core"), ("x", "yl")
    placed = (P(pair, None, pw), P(pair, None, pw), P(pw))
    return jax.shard_map(
        body, mesh=fine, in_specs=placed, out_specs=P(pair, None, pw, None), check_vma=False
    )
```

```python
import functools

import jax
import jax.numpy as jnp
from jax import lax
from jax.experimental import pallas as pl
from jax.experimental.pallas import tpu as pltpu
from jax.sharding import Mesh, PartitionSpec as P

BF16 = jnp.bfloat16
F32 = jnp.float32
AXES = ("x", "yl", "yh", "z", "core")
SIZES = (4, 2, 4, 8, 2)
NX, NL, NH, NZ, NC = SIZES
NQ = NX * NL
LANES = 128
MIB = 2**20
LONG = 10**11


def along(block, step):
    return lax.ppermute(block, "yh", [(i, (i + step) % NH) for i in range(NH)])


def dot(left, right):
    return lax.dot_general(left, right, (((1,), (1,)), ((), ())), preferred_element_type=F32)


def mark_kernel(seen_ref, out_ref):
    out_ref[...] = seen_ref[...]


def mark(seen):
    return pl.pallas_call(
        mark_kernel,
        out_shape=jax.ShapeDtypeStruct(seen.shape, seen.dtype),
        compiler_params=pltpu.CompilerParams(vmem_limit_bytes=MIB),
        cost_estimate=pl.CostEstimate(flops=LONG, bytes_accessed=10**8, transcendentals=0),
    )(seen)


def product_kernel(sides, cuts, ignored, at_row, *refs):
    pieces, width = sum(cuts), len(sides)
    rows_refs, piece_refs = refs[:width], list(refs[width : width + pieces])
    out_ref, held, out_sem = refs[width + pieces + ignored :]
    core = lax.axis_index("core")
    nz, rows, planes = rows_refs[0].shape
    wide = rows // NQ
    parts = [ref[...].reshape(nz * rows, planes) for ref in rows_refs]
    whole = parts[0] if width == 1 else jnp.concatenate(parts, axis=0)
    done = []
    for cut in cuts:
        group = [piece_refs.pop(0)[...] for _ in range(cut)]
        block = group[0] if cut == 1 else jnp.concatenate(group, axis=0)
        term = dot(whole, block)
        done += [term[:, c : c + LANES] for c in range(0, term.shape[1], LANES)]
    tall = held.shape[3]
    copies = []
    for n, side in enumerate(sides):
        for zi in range(nz):
            for qi in range(NQ):
                at = (n * nz + zi) * rows + qi * wide
                block = jnp.concatenate([d[at : at + wide] for d in done], axis=0)
                held[n, qi, zi] = block.astype(BF16)
        owner = core if side == 0 else 1 - core
        target = out_ref.at[:, :, owner, pl.ds(at_row, tall)]
        copies.append(pltpu.make_async_copy(held.at[n], target, out_sem.at[n]))
        copies[-1].start()
    for copy in copies:
        copy.wait()


def product(lefts, sides, blocks, at_row, height, unread=(), begun=None, flops=None):
    nz, rows, width = lefts[0].shape
    wide = rows // NQ
    cuts = tuple(len(block) for block in blocks)
    columns = sum(piece.shape[0] for piece in blocks[0])
    count = len(blocks)
    tall = count * columns // LANES * wide
    if flops is None:
        flops = 2 * len(lefts) * nz * rows * width * columns * count
    near = pl.BlockSpec(memory_space=pltpu.VMEM)
    anywhere = pl.BlockSpec(memory_space=pl.ANY)
    operands = [*lefts, *[piece for block in blocks for piece in block], *unread]
    ignored, aliases = len(unread), {}
    if begun is not None:
        aliases = {len(operands): 0}
        operands.append(begun)
        ignored += 1
    return pl.pallas_call(
        functools.partial(product_kernel, sides, cuts, ignored, at_row),
        out_shape=jax.ShapeDtypeStruct((NQ, nz, NC, height, LANES), BF16),
        in_specs=[near] * (len(lefts) + sum(cuts)) + [anywhere] * ignored,
        out_specs=pl.BlockSpec(memory_space=pl.ANY),
        scratch_shapes=[
            pltpu.VMEM((len(lefts), NQ, nz, tall, LANES), BF16),
            pltpu.SemaphoreType.DMA((len(lefts),)),
        ],
        input_output_aliases=aliases,
        compiler_params=pltpu.CompilerParams(vmem_limit_bytes=14 * MIB),
        cost_estimate=pl.CostEstimate(flops=flops, bytes_accessed=5 * MIB, transcendentals=0),
    )(*operands)


def add_kernel(*refs):
    out_ref, at = refs[-1], 0
    for ref in refs[:-1]:
        total = ref[0].astype(F32)
        for qi in range(1, NQ):
            total = total + ref[qi].astype(F32)
        tall = total.shape[1]
        out_ref[:, at : at + tall] = total.astype(BF16)
        at += tall


def add(*terms):
    rest = terms[0].shape[1]
    tall = sum(t.shape[2] for t in terms)
    step = rest // 4
    return pl.pallas_call(
        add_kernel,
        grid=(rest // step,),
        out_shape=jax.ShapeDtypeStruct((rest, tall, LANES), BF16),
        in_specs=[
            pl.BlockSpec((NQ, step, t.shape[2], LANES), lambda i: (0, i, 0, 0)) for t in terms
        ],
        out_specs=pl.BlockSpec((step, tall, LANES), lambda i: (i, 0, 0)),
        compiler_params=pltpu.CompilerParams(vmem_limit_bytes=8 * MIB),
        cost_estimate=pl.CostEstimate(flops=MIB, bytes_accessed=2 * MIB, transcendentals=0),
    )(*terms)


def finish_kernel(terms_ref, out_ref):
    yh = lax.axis_index("yh")
    wide, columns = out_ref.shape[2:]
    values = terms_ref[...].astype(F32)
    at = 0
    for offset in (0, NH - 1, 1, 2):
        owner = lax.rem(yh + offset, NH)
        for c in range(0, columns, LANES):
            out_ref[owner, :, :, c : c + LANES] = values[:, at : at + wide]
            at += wide


def finish(terms, columns):
    rest, tall, _ = terms.shape
    wide = tall * LANES // columns // NH
    step = rest // 2
    return pl.pallas_call(
        finish_kernel,
        grid=(rest // step,),
        out_shape=jax.ShapeDtypeStruct((NH, rest, wide, columns), F32),
        in_specs=[pl.BlockSpec((step, tall, LANES), lambda i: (i, 0, 0))],
        out_specs=pl.BlockSpec((NH, step, wide, columns), lambda i: (0, i, 0, 0)),
        compiler_params=pltpu.CompilerParams(vmem_limit_bytes=8 * MIB),
        cost_estimate=pl.CostEstimate(flops=2**17, bytes_accessed=MIB, transcendentals=0),
    )(terms)


def body(valence_pairs, conduction_pairs, screening):
    _, second, plane_dev = valence_pairs.shape
    own = conduction_pairs[0]
    columns = own.shape[0]
    cut = columns // 4

    ahead, back = along(own, 1), along(own, NH - 1)

    screened = (valence_pairs[0].astype(F32) * screening[None, :]).astype(BF16)
    sent = jnp.broadcast_to(screened[None], (NZ, second, plane_dev))
    mine = lax.all_to_all(sent, "z", 0, 0, tiled=True)
    mine, *rows = lax.optimization_barrier((mine, back[:16], ahead[:16], mark(screening[None])))
    other = lax.ppermute(mine, "core", [(0, 1), (1, 0)])

    far = along(ahead[:cut], 1), along(back[cut:], NH - 1)

    height = NH * columns // LANES * (second // NQ)
    most = (NH - 1) * columns // LANES * (second // NQ)
    near = ((own,), (ahead,), (back,))
    terms = product([mine], (0,), near, 0, height, rows, None, LONG)
    terms = product([other], (1,), near, 0, height, (), terms)
    terms = product([mine, other], (0, 1), (far,), most, height, (), terms)
    terms = terms.reshape(NQ, NZ * NC, height, LANES)
    terms = lax.all_to_all(terms, ("x", "yl"), 0, 0, tiled=True)
    terms = lax.all_to_all(add(terms), ("z", "core"), 0, 0, tiled=True)
    out = finish(terms, columns)
    return out.reshape(1, NH * NZ * NC, second // NQ, columns)


def solution(mesh):
    fine = Mesh(mesh.devices.reshape(SIZES), AXES)
    pair, pw = ("yh", "z", "core"), ("x", "yl")
    placed = (P(pair, None, pw), P(pair, None, pw), P(pw))
    return jax.shard_map(
        body, mesh=fine, in_specs=placed, out_specs=P(pair, None, pw, None), check_vma=False
    )
```
